128 devices in a mesh: dp: 2 (over core), seq: 16 (over y, z), tensor: 4 (over x).
Axes of the slice: x: 4, y: 4, z: 4, core: 2. Of those that a mesh axis runs over, the one named last changes fastest.
Arguments:
- block_input: bfloat16 [2, 4096, 1024], P('dp', 'seq'), may hold values from -6 to 6
- upstream_grad: bfloat16 [2, 4096, 1024], P('dp', 'seq'), may hold values from -6 to 6
- query_weight: float32 [1024, 1024], P(('dp', 'seq'), 'tensor'), may hold values from -0.1875 to 0.1875
- key_value_weight: float32 [1024, 2, 512], P(('dp', 'seq'), None, 'tensor'), may hold values from -0.1875 to 0.1875
- output_weight: float32 [1024, 1024], P(('dp', 'seq'), 'tensor'), may hold values from -4 to 4
- gateup_weight: float32 [1024, 2, 4608], P(('dp', 'seq'), None, 'tensor'), may hold values from -0.1875 to 0.1875
- down_weight: float32 [1024, 4608], P(('dp', 'seq'), 'tensor'), may hold values from -0.09375 to 0.09375
- norm_gains: float32 [1024, 2], P(('dp', 'seq')), may hold values from 0.5 to 1.5
- head_norm_gains: float32 [2, 64], replicated, may hold values from 0.6 to 1.6
- query_momentum: float32 [1024, 1024], P(('dp', 'seq'), 'tensor'), may hold values from -5.43058 to 5.43058
- query_variance: float32 [1024, 1024], P(('dp', 'seq'), 'tensor'), may hold values from 1556.48 to 6225.92
- key_value_momentum: float32 [1024, 2, 512], P(('dp', 'seq'), None, 'tensor'), may hold values from -5.43058 to 5.43058
- key_value_variance: float32 [1024, 2, 512], P(('dp', 'seq'), None, 'tensor'), may hold values from 1556.48 to 6225.92
- output_momentum: float32 [1024, 1024], P(('dp', 'seq'), 'tensor'), may hold values from -10.86116 to 10.86116
- output_variance: float32 [1024, 1024], P(('dp', 'seq'), 'tensor'), may hold values from 12.288 to 49.152
- gateup_momentum: float32 [1024, 2, 4608], P(('dp', 'seq'), None, 'tensor'), may hold values from -13.57645 to 13.57645
- gateup_variance: float32 [1024, 2, 4608], P(('dp', 'seq'), None, 'tensor'), may hold values from 81.92 to 327.68
- down_momentum: float32 [1024, 4608], P(('dp', 'seq'), 'tensor'), may hold values from -32.58348 to 32.58348
- down_variance: float32 [1024, 4608], P(('dp', 'seq'), 'tensor'), may hold values from 491.52 to 1966.08
- norm_momentum: float32 [1024, 2], P(('dp', 'seq')), may hold values from -54.3058 to 54.3058
- norm_variance: float32 [1024, 2], P(('dp', 'seq')), may hold values from 9830.4 to 39321.6
- head_momentum: float32 [2, 64], replicated, may hold values from -86.88928 to 86.88928
- head_variance: float32 [2, 64], replicated, may hold values from 39321 to 157286
Outputs:
- block_output: bfloat16 [2, 4096, 1024], P('dp', 'seq')
- input_grad: float32 [2, 4096, 1024], P('dp', 'seq')
- query_grad: float32 [1024, 1024], P(('dp', 'seq'), 'tensor')
- keyvalue_grad: float32 [1024, 2, 512], P(('dp', 'seq'), None, 'tensor')
- output_grad: float32 [1024, 1024], P(('dp', 'seq'), 'tensor')
- gateup_grad: float32 [1024, 2, 4608], P(('dp', 'seq'), None, 'tensor')
- down_grad: float32 [1024, 4608], P(('dp', 'seq'), 'tensor')
- norm_grad: float32 [1024, 2], P(('dp', 'seq'))
- head_grad: float32 [2, 64], replicated
- query_direction: float32 [1024, 1024], P(('dp', 'seq'), 'tensor')
- keyvalue_direction: float32 [1024, 2, 512], P(('dp', 'seq'), None, 'tensor')
- output_direction: float32 [1024, 1024], P(('dp', 'seq'), 'tensor')
- gateup_direction: float32 [1024, 2, 4608], P(('dp', 'seq'), None, 'tensor')
- down_direction: float32 [1024, 4608], P(('dp', 'seq'), 'tensor')
- norm_direction: float32 [1024, 2], P(('dp', 'seq'))
- head_direction: float32 [2, 64], replicated
- query_first: float32 [1024, 1024], P(('dp', 'seq'), 'tensor')
- query_second: float32 [1024, 1024], P(('dp', 'seq'), 'tensor')
- keyvalue_first: float32 [1024, 2, 512], P(('dp', 'seq'), None, 'tensor')
- keyvalue_second: float32 [1024, 2, 512], P(('dp', 'seq'), None, 'tensor')
- output_first: float32 [1024, 1024], P(('dp', 'seq'), 'tensor')
- output_second: float32 [1024, 1024], P(('dp', 'seq'), 'tensor')
- gateup_first: float32 [1024, 2, 4608], P(('dp', 'seq'), None, 'tensor')
- gateup_second: float32 [1024, 2, 4608], P(('dp', 'seq'), None, 'tensor')
- down_first: float32 [1024, 4608], P(('dp', 'seq'), 'tensor')
- down_second: float32 [1024, 4608], P(('dp', 'seq'), 'tensor')
- norm_first: float32 [1024, 2], P(('dp', 'seq'))
- norm_second: float32 [1024, 2], P(('dp', 'seq'))
- head_first: float32 [2, 64], replicated
- head_second: float32 [2, 64], replicated
The draws below stay inside these ranges and needn't reach their ends.
All inputs are finite; a program needn't handle non-finite values.
Results may differ from the reference program's by a relative error of at most 0.025.
Values may be sent and summed in bfloat16 or wider, within the bound.
A program may use at most 128 MiB of HBM per device.

```python
import math
import jax
import jax.numpy as jnp
from jax import lax

MODEL_WIDTH = 1024
QUERY_HEADS = 16
KEY_VALUE_HEADS = 8
HEAD_SIZE = 64
FF = 4608
LEN = 4096
SEQS = 2


def draw_head_norm_gains(key, part):
    return jax.random.uniform(key, (2, HEAD_SIZE), jnp.float32, 0.6, 1.6)


def shard_levels(own_key, shape, cuts, least, largest):
    gain, own = 1.0, jax.random.fold_in(own_key, 6)
    for position, parts in cuts:
        steps = jnp.exp(jax.random.uniform(jax.random.fold_in(own, position), (parts,), jnp.float32, least / len(cuts), largest / len(cuts)))
        gain = gain * jnp.repeat(steps, shape[position] // parts).reshape([-1 if axis == position else 1 for axis in range(len(shape))])
    return gain


def normal_values(stream_key, extent, spread, bound, cuts=(), kind=jnp.bfloat16):
    loudness = shard_levels(stream_key, extent, cuts, -0.22, 0.18) if cuts else 1.0
    values = jax.random.normal(stream_key, extent, jnp.float32) * spread * loudness
    return jnp.minimum(jnp.maximum(values, -bound), bound).astype(kind)


def setup_inputs(seed: int = 0) -> dict:
    seeds = jax.random.split(jax.random.key(seed), 24)
    block_input = normal_values(seeds[0], (SEQS, LEN, MODEL_WIDTH), 1.0, 6.0, ((0, 2), (1, 16)))
    upstream_grad = normal_values(seeds[1], (SEQS, LEN, MODEL_WIDTH), 1.0, 6.0, ((0, 2), (1, 16)))
    query_weight = normal_values(seeds[2], (MODEL_WIDTH, QUERY_HEADS * HEAD_SIZE), MODEL_WIDTH ** -0.5, 0.1875, ((0, 32), (1, 4)), jnp.float32)
    key_value_weight = normal_values(seeds[3], (MODEL_WIDTH, 2, KEY_VALUE_HEADS * HEAD_SIZE), MODEL_WIDTH ** -0.5, 0.1875, ((0, 32), (2, 4)), jnp.float32)
    output_weight = normal_values(seeds[4], (MODEL_WIDTH, QUERY_HEADS * HEAD_SIZE), 2 ** -0.5, 4.0, ((0, 32), (1, 4)), jnp.float32)
    gateup_weight = normal_values(seeds[5], (MODEL_WIDTH, 2, FF), MODEL_WIDTH ** -0.5, 0.1875, ((0, 32), (2, 4)), jnp.float32)
    down_weight = normal_values(seeds[6], (MODEL_WIDTH, FF), FF ** -0.5, 0.09375, ((0, 32), (1, 4)), jnp.float32)
    norm_gains = jnp.clip(1.0 + 0.1 * jax.random.normal(seeds[7], (MODEL_WIDTH, 2), jnp.float32), 0.5, 1.5)
    head_norm_gains = draw_head_norm_gains(jax.random.fold_in(seeds[23], 71), 0)
    query_momentum = normal_values(seeds[9], (MODEL_WIDTH, QUERY_HEADS * HEAD_SIZE), (0.01 * (SEQS * LEN) ** 0.5), 5.43058, ((0, 32), (1, 4)), jnp.float32)
    query_variance = jnp.clip(jnp.exp(math.log(6225.92) - 1.3862944 * jax.random.uniform(seeds[10], (MODEL_WIDTH, QUERY_HEADS * HEAD_SIZE), jnp.float32) ** shard_levels(seeds[10], (MODEL_WIDTH, QUERY_HEADS * HEAD_SIZE), ((0, 32), (1, 4)), -0.2, 0.2)), 1556.48, 6225.92)
    key_value_momentum = normal_values(seeds[11], (MODEL_WIDTH, 2, KEY_VALUE_HEADS * HEAD_SIZE), (0.01 * (SEQS * LEN) ** 0.5), 5.43058, ((0, 32), (2, 4)), jnp.float32)
    key_value_variance = jnp.clip(jnp.exp(math.log(6225.92) - 1.3862944 * jax.random.uniform(seeds[12], (MODEL_WIDTH, 2, KEY_VALUE_HEADS * HEAD_SIZE), jnp.float32) ** shard_levels(seeds[12], (MODEL_WIDTH, 2, KEY_VALUE_HEADS * HEAD_SIZE), ((0, 32), (2, 4)), -0.2, 0.2)), 1556.48, 6225.92)
    output_momentum = normal_values(seeds[13], (MODEL_WIDTH, QUERY_HEADS * HEAD_SIZE), (0.02 * (SEQS * LEN) ** 0.5), 10.86116, ((0, 32), (1, 4)), jnp.float32)
    output_variance = jnp.clip(jnp.exp(math.log(49.152) - 1.3862944 * jax.random.uniform(seeds[14], (MODEL_WIDTH, QUERY_HEADS * HEAD_SIZE), jnp.float32) ** shard_levels(seeds[14], (MODEL_WIDTH, QUERY_HEADS * HEAD_SIZE), ((0, 32), (1, 4)), -0.2, 0.2)), 12.288, 49.152)
    gateup_momentum = normal_values(seeds[15], (MODEL_WIDTH, 2, FF), (0.025 * (SEQS * LEN) ** 0.5), 13.57645, ((0, 32), (2, 4)), jnp.float32)
    gateup_variance = jnp.clip(jnp.exp(math.log(327.68) - 1.3862944 * jax.random.uniform(seeds[16], (MODEL_WIDTH, 2, FF), jnp.float32) ** shard_levels(seeds[16], (MODEL_WIDTH, 2, FF), ((0, 32), (2, 4)), -0.2, 0.2)), 81.92, 327.68)
    down_momentum = normal_values(seeds[17], (MODEL_WIDTH, FF), (0.06 * (SEQS * LEN) ** 0.5), 32.58348, ((0, 32), (1, 4)), jnp.float32)
    down_variance = jnp.clip(jnp.exp(math.log(1966.08) - 1.3862944 * jax.random.uniform(seeds[18], (MODEL_WIDTH, FF), jnp.float32) ** shard_levels(seeds[18], (MODEL_WIDTH, FF), ((0, 32), (1, 4)), -0.2, 0.2)), 491.52, 1966.08)
    norm_momentum = normal_values(seeds[19], (MODEL_WIDTH, 2), (0.1 * (SEQS * LEN) ** 0.5), 54.3058, ((0, 32),), jnp.float32)
    norm_variance = jnp.clip(jnp.exp(math.log(39321.6) - 1.3862944 * jax.random.uniform(seeds[20], (MODEL_WIDTH, 2), jnp.float32) ** shard_levels(seeds[20], (MODEL_WIDTH, 2), ((0, 32),), -0.2, 0.2)), 9830.4, 39321.6)
    head_momentum = normal_values(seeds[21], (2, HEAD_SIZE), (0.04 * (SEQS * LEN * QUERY_HEADS) ** 0.5), 86.88928, (), jnp.float32)
    head_variance = jnp.clip(jnp.exp(jax.random.uniform(seeds[22], (2, HEAD_SIZE), jnp.float32, math.log(39321.0), math.log(157286.0))), 39321.0, 157286.0)
    return {"block_input": block_input, "upstream_grad": upstream_grad, "query_weight": query_weight, "key_value_weight": key_value_weight, "output_weight": output_weight, "gateup_weight": gateup_weight, "down_weight": down_weight, "norm_gains": norm_gains, "head_norm_gains": head_norm_gains, "query_momentum": query_momentum, "query_variance": query_variance, "key_value_momentum": key_value_momentum, "key_value_variance": key_value_variance, "output_momentum": output_momentum, "output_variance": output_variance, "gateup_momentum": gateup_momentum, "gateup_variance": gateup_variance, "down_momentum": down_momentum, "down_variance": down_variance, "norm_momentum": norm_momentum, "norm_variance": norm_variance, "head_momentum": head_momentum, "head_variance": head_variance}


norm_eps = 1e-05
rope_base = 1000000.0
beta_one = 0.9
beta_two = 0.95
adam_eps = 1e-08
decay_rate = 0.1
adam_count = 3
masked_score = -1e+30

def round_half(values):
    return lax.optimization_barrier(values.astype(jnp.bfloat16)).astype(jnp.float32)

def rms_forward(values, gain_row):
    inverse = lax.rsqrt(lax.optimization_barrier(jnp.mean(values * values, axis=-1, keepdims=True)) + norm_eps)
    normed = values * inverse
    return (normed * gain_row, normed, inverse)

def root_mean_square_backward(grad_out, gain_row, normed, inverse):
    grad_normed = grad_out * gain_row
    inner_mean = lax.optimization_barrier(jnp.mean(grad_normed * normed, axis=-1, keepdims=True))
    return inverse * (grad_normed - normed * inner_mean)

def rope_tables(positions, head_width):
    half_width = head_width // 2
    frequency = rope_base ** (-(jnp.arange(half_width, dtype=jnp.float32) * 2.0) / head_width)
    angles = positions.astype(jnp.float32)[:, None] * frequency[None, :]
    return (jnp.cos(angles), jnp.sin(angles))

def rotate(values, cosine, sine_table):
    half_width = values.shape[-1] // 2
    first_half = values[..., :half_width]
    second_half = values[..., half_width:]
    cos_rows = cosine[:, None, :]
    sin_rows = sine_table[:, None, :]
    return jnp.concatenate([first_half * cos_rows - second_half * sin_rows, second_half * cos_rows + first_half * sin_rows], axis=-1)

def rotate_back(gradient, cosine, sine_table):
    half_width = gradient.shape[-1] // 2
    first_half = gradient[..., :half_width]
    second_half = gradient[..., half_width:]
    cos_rows = cosine[:, None, :]
    sin_rows = sine_table[:, None, :]
    return jnp.concatenate([first_half * cos_rows + second_half * sin_rows, second_half * cos_rows - first_half * sin_rows], axis=-1)

def contract_rows(left, right):
    return lax.dot_general(left, right, (((0,), (0,)), ((), ())), preferred_element_type=jnp.float32)

def contract_cols(left, right):
    return lax.dot_general(left, right, (((1,), (1,)), ((), ())), preferred_element_type=jnp.float32)

def attend_forward(query_half16, key16, value_half16):
    sequence_length = query_half16.shape[0]
    rows_per_block = 512 if sequence_length % 512 == 0 else sequence_length
    group_count = QUERY_HEADS // KEY_VALUE_HEADS
    factor = 1.0 / HEAD_SIZE ** 0.5
    keys = key16.astype(jnp.float32)
    values = value_half16.astype(jnp.float32)
    key_pos = jnp.arange(sequence_length, dtype=jnp.int32)

    def one_block(block_index):
        starting_row = (block_index * rows_per_block).astype(jnp.int32)
        query_block = lax.dynamic_slice_in_dim(query_half16, starting_row, rows_per_block, 0).astype(jnp.float32).reshape(rows_per_block, KEY_VALUE_HEADS, group_count, HEAD_SIZE)
        scores = jnp.einsum('qhgd,khd->hgqk', query_block, keys) * factor
        causal = key_pos[None, :] <= (starting_row + jnp.arange(rows_per_block, dtype=jnp.int32))[:, None]
        scores = jnp.where(causal, scores, masked_score)
        row_max = lax.optimization_barrier(jnp.max(scores, axis=-1, keepdims=True))
        exp_scores = jnp.exp(scores - row_max)
        totals = lax.optimization_barrier(jnp.sum(exp_scores, axis=-1))
        mixed = jnp.einsum('hgqk,khd->hgqd', round_half(exp_scores), values)
        output = (mixed / totals[..., None]).transpose(2, 0, 1, 3).reshape(rows_per_block, QUERY_HEADS, HEAD_SIZE)
        return (output.astype(jnp.bfloat16), row_max[..., 0] + jnp.log(totals))
    outputs, log_total = lax.map(one_block, jnp.arange(sequence_length // rows_per_block, dtype=jnp.int32))
    return (outputs.reshape(sequence_length, QUERY_HEADS, HEAD_SIZE), log_total)

def attend_backward(query_half16, key16, value_half16, output_half16, log_total, gradient_half16):
    sequence_length = query_half16.shape[0]
    rows_per_block = 512 if sequence_length % 512 == 0 else sequence_length
    group_count = QUERY_HEADS // KEY_VALUE_HEADS
    factor = 1.0 / HEAD_SIZE ** 0.5
    keys = key16.astype(jnp.float32)
    values = value_half16.astype(jnp.float32)
    key_pos = jnp.arange(sequence_length, dtype=jnp.int32)

    def one_block(carried, block_index):
        grad_keys, grad_values = carried
        starting_row = (block_index * rows_per_block).astype(jnp.int32)
        query_block = lax.dynamic_slice_in_dim(query_half16, starting_row, rows_per_block, 0).astype(jnp.float32).reshape(rows_per_block, KEY_VALUE_HEADS, group_count, HEAD_SIZE)
        gradient_block = lax.dynamic_slice_in_dim(gradient_half16, starting_row, rows_per_block, 0).astype(jnp.float32).reshape(rows_per_block, KEY_VALUE_HEADS, group_count, HEAD_SIZE)
        output_block = lax.dynamic_slice_in_dim(output_half16, starting_row, rows_per_block, 0).astype(jnp.float32).reshape(rows_per_block, KEY_VALUE_HEADS, group_count, HEAD_SIZE)
        delta = lax.optimization_barrier(jnp.sum(gradient_block * output_block, axis=-1)).transpose(1, 2, 0)
        scores = jnp.einsum('qhgd,khd->hgqk', query_block, keys) * factor
        causal = key_pos[None, :] <= (starting_row + jnp.arange(rows_per_block, dtype=jnp.int32))[:, None]
        scores = jnp.where(causal, scores, masked_score)
        probs = jnp.where(causal, jnp.exp(scores - log_total[block_index][..., None]), 0.0)
        grad_values = grad_values + jnp.einsum('hgqk,qhgd->khd', round_half(probs), gradient_block)
        grad_probs = jnp.einsum('qhgd,khd->hgqk', gradient_block, values)
        grad_scores = round_half(probs * (grad_probs - delta[..., None]))
        grad_query = jnp.einsum('hgqk,khd->qhgd', grad_scores, keys) * factor
        grad_keys = grad_keys + jnp.einsum('hgqk,qhgd->khd', grad_scores, query_block) * factor
        return ((grad_keys, grad_values), grad_query.reshape(rows_per_block, QUERY_HEADS, HEAD_SIZE))
    blank_start = jnp.zeros((sequence_length, KEY_VALUE_HEADS, HEAD_SIZE), jnp.float32)
    (grad_keys, grad_values), grad_query = lax.scan(one_block, (blank_start, blank_start), jnp.arange(sequence_length // rows_per_block, dtype=jnp.int32))
    return (grad_query.reshape(sequence_length, QUERY_HEADS, HEAD_SIZE), grad_keys, grad_values)

def one_sequence(input16, upstream16, weights, head_norm_gains):
    query_matrix, key_value_matrix, output_matrix, gateup_matrix, down_matrix, gain_table = weights
    sequence_length = input16.shape[0]
    gain_one = gain_table[:, 0]
    gain_two = gain_table[:, 1]
    resid_in = input16.astype(jnp.float32)
    first_norm, normed_one, inverse_one = rms_forward(resid_in, gain_one)
    hidden_first = first_norm.astype(jnp.bfloat16)
    query = jnp.dot(hidden_first, query_matrix, preferred_element_type=jnp.float32).reshape(sequence_length, QUERY_HEADS, HEAD_SIZE)
    key_unnormed = jnp.dot(hidden_first, key_value_matrix[:, 0, :], preferred_element_type=jnp.float32).reshape(sequence_length, KEY_VALUE_HEADS, HEAD_SIZE)
    value_half16 = jnp.dot(hidden_first, key_value_matrix[:, 1, :], preferred_element_type=jnp.float32).astype(jnp.bfloat16).reshape(sequence_length, KEY_VALUE_HEADS, HEAD_SIZE)
    query_norm, query_hat, query_inverse = rms_forward(query, head_norm_gains[0])
    key_norm, key_normalized, key_inverse_norm = rms_forward(key_unnormed, head_norm_gains[1])
    cosine, sine_table = rope_tables(jnp.arange(sequence_length, dtype=jnp.int32), HEAD_SIZE)
    query_half16 = rotate(query_norm, cosine, sine_table).astype(jnp.bfloat16)
    key16 = rotate(key_norm, cosine, sine_table).astype(jnp.bfloat16)
    output_half16, log_total = attend_forward(query_half16, key16, value_half16)
    out_flat = output_half16.reshape(sequence_length, QUERY_HEADS * HEAD_SIZE)
    resid_mid = resid_in + contract_cols(out_flat, output_matrix)
    second_norm, normed_two, inverse_two = rms_forward(resid_mid, gain_two)
    hidden_two = second_norm.astype(jnp.bfloat16)
    gate = jnp.dot(hidden_two, gateup_matrix[:, 0, :], preferred_element_type=jnp.float32)
    upward = jnp.dot(hidden_two, gateup_matrix[:, 1, :], preferred_element_type=jnp.float32)
    sigmoid_gate = jax.nn.sigmoid(gate)
    silu_gate = gate * sigmoid_gate
    inner16 = (silu_gate * upward).astype(jnp.bfloat16)
    output = (resid_mid + contract_cols(inner16, down_matrix)).astype(jnp.bfloat16)
    grad_down = contract_rows(upstream16, inner16)
    grad_inner = jnp.dot(upstream16, down_matrix, preferred_element_type=jnp.float32)
    grad_gate16 = (grad_inner * upward * sigmoid_gate * (1.0 + gate * (1.0 - sigmoid_gate))).astype(jnp.bfloat16)
    grad_up16 = (grad_inner * silu_gate).astype(jnp.bfloat16)
    grad_gateup = jnp.stack([contract_rows(hidden_two, grad_gate16), contract_rows(hidden_two, grad_up16)], axis=1)
    grad_hidden_two = contract_cols(grad_gate16, gateup_matrix[:, 0, :]) + contract_cols(grad_up16, gateup_matrix[:, 1, :])
    grad_mid = upstream16.astype(jnp.float32) + root_mean_square_backward(grad_hidden_two, gain_two, normed_two, inverse_two)
    grad_mid16 = grad_mid.astype(jnp.bfloat16)
    grad_output = contract_rows(grad_mid16, out_flat)
    grad_out16 = jnp.dot(grad_mid16, output_matrix, preferred_element_type=jnp.float32).astype(jnp.bfloat16).reshape(sequence_length, QUERY_HEADS, HEAD_SIZE)
    grad_query, key_gradient, value_gradient = attend_backward(query_half16, key16, value_half16, output_half16, log_total, grad_out16)
    grad_query = rotate_back(grad_query, cosine, sine_table)
    key_gradient = rotate_back(key_gradient, cosine, sine_table)
    grad_heads = jnp.stack([lax.optimization_barrier(jnp.sum(grad_query * query_hat, axis=(0, 1))), lax.optimization_barrier(jnp.sum(key_gradient * key_normalized, axis=(0, 1)))], axis=0)
    grad_query16 = root_mean_square_backward(grad_query, head_norm_gains[0], query_hat, query_inverse).reshape(sequence_length, QUERY_HEADS * HEAD_SIZE).astype(jnp.bfloat16)
    key_gradient16 = root_mean_square_backward(key_gradient, head_norm_gains[1], key_normalized, key_inverse_norm).reshape(sequence_length, KEY_VALUE_HEADS * HEAD_SIZE).astype(jnp.bfloat16)
    value_gradient16 = value_gradient.reshape(sequence_length, KEY_VALUE_HEADS * HEAD_SIZE).astype(jnp.bfloat16)
    grad_querymat = contract_rows(hidden_first, grad_query16)
    grad_keyvalue = jnp.stack([contract_rows(hidden_first, key_gradient16), contract_rows(hidden_first, value_gradient16)], axis=1)
    grad_hidden_one = contract_cols(grad_query16, query_matrix) + contract_cols(key_gradient16, key_value_matrix[:, 0, :]) + contract_cols(value_gradient16, key_value_matrix[:, 1, :])
    grad_input = grad_mid + root_mean_square_backward(grad_hidden_one, gain_one, normed_one, inverse_one)
    grad_gains = jnp.stack([lax.optimization_barrier(jnp.sum(grad_hidden_one * normed_one, axis=0)), lax.optimization_barrier(jnp.sum(grad_hidden_two * normed_two, axis=0))], axis=1)
    return (output, grad_input, (grad_querymat, grad_keyvalue, grad_output, grad_gateup, grad_down, grad_gains, grad_heads))

def adamw(weight, momentum, variance, gradient, decay):
    first = beta_one * momentum + (1.0 - beta_one) * gradient
    second = beta_two * variance + (1.0 - beta_two) * gradient * gradient
    first_fixed = first / (1.0 - beta_one ** adam_count)
    second_fixed = second / (1.0 - beta_two ** adam_count)
    direction = first_fixed / (jnp.sqrt(second_fixed) + adam_eps) + decay * weight
    return (direction, first, second)

def reference(block_input, upstream_grad, query_weight, key_value_weight, output_weight, gateup_weight, down_weight, norm_gains, head_norm_gains, query_momentum, query_variance, key_value_momentum, key_value_variance, output_momentum, output_variance, gateup_momentum, gateup_variance, down_momentum, down_variance, norm_momentum, norm_variance, head_momentum, head_variance):
    weights = (query_weight.astype(jnp.bfloat16), key_value_weight.astype(jnp.bfloat16), output_weight.astype(jnp.bfloat16), gateup_weight.astype(jnp.bfloat16), down_weight.astype(jnp.bfloat16), norm_gains.astype(jnp.bfloat16).astype(jnp.float32))
    zero_filled = (jnp.zeros(query_weight.shape, jnp.float32), jnp.zeros(key_value_weight.shape, jnp.float32), jnp.zeros(output_weight.shape, jnp.float32), jnp.zeros(gateup_weight.shape, jnp.float32), jnp.zeros(down_weight.shape, jnp.float32), jnp.zeros(norm_gains.shape, jnp.float32), jnp.zeros(head_norm_gains.shape, jnp.float32))

    def per_sequence(totals, pair):
        output, grad_input, grads = one_sequence(pair[0], pair[1], weights, head_norm_gains)
        return (jax.tree.map(lambda left, right: left + right, totals, grads), (output, grad_input))
    totals, (outputs, input_grads) = lax.scan(per_sequence, zero_filled, (block_input, upstream_grad))
    grad_q, grad_kv, grad_o, grad_gu, grad_d, grad_n, grad_h = totals
    new_q = adamw(query_weight, query_momentum, query_variance, grad_q, decay_rate)
    new_kv = adamw(key_value_weight, key_value_momentum, key_value_variance, grad_kv, decay_rate)
    new_o = adamw(output_weight, output_momentum, output_variance, grad_o, decay_rate)
    new_gu = adamw(gateup_weight, gateup_momentum, gateup_variance, grad_gu, decay_rate)
    new_d = adamw(down_weight, down_momentum, down_variance, grad_d, decay_rate)
    new_n = adamw(norm_gains, norm_momentum, norm_variance, grad_n, 0.0)
    new_h = adamw(head_norm_gains, head_momentum, head_variance, grad_h, 0.0)
    return (outputs, input_grads, grad_q, grad_kv, grad_o, grad_gu, grad_d, grad_n, grad_h, new_q[0], new_kv[0], new_o[0], new_gu[0], new_d[0], new_n[0], new_h[0], new_q[1], new_q[2], new_kv[1], new_kv[2], new_o[1], new_o[2], new_gu[1], new_gu[2], new_d[1], new_d[2], new_n[1], new_n[2], new_h[1], new_h[2])
```

```python
import functools

import jax
import jax.numpy as jnp
from jax import lax
from jax.experimental import pallas as pl
from jax.experimental.pallas import tpu as pltpu
from jax.sharding import PartitionSpec as P

f32 = jnp.float32
bf16 = jnp.bfloat16
MESH = pl.DeviceIdType.MESH
norm_eps = 1e-05
rope_base = 1000000.0
beta_one = 0.9
beta_two = 0.95
adam_eps = 1e-08
decay_rate = 0.1
adam_count = 3
LOG2E = 1.4426950408889634
ROWS = 256
HD = 64
SCALE = 0.125
CA = 896
CF = 3456
FFC = 1152
SPLIT_A = 512
SPLIT_F = 1792
VMEM = pl.BlockSpec(memory_space=pltpu.VMEM)
ANY = pl.BlockSpec(memory_space=pl.ANY)


def params(collective_id, megabytes=56):
    return pltpu.CompilerParams(
        collective_id=collective_id,
        has_side_effects=True,
        vmem_limit_bytes=megabytes * 1024 * 1024,
    )


def remote(src, dst, send_sem, recv_sem, device):
    return pltpu.make_async_remote_copy(
        src_ref=src,
        dst_ref=dst,
        send_sem=send_sem,
        recv_sem=recv_sem,
        device_id=device,
        device_id_type=MESH,
    )


def transposed(x, dtype):
    return x.astype(f32).T.astype(dtype)


def dot_nt(a, b):
    return lax.dot_general(a, b, (((1,), (1,)), ((), ())), preferred_element_type=f32)


def dot_nn(a, b):
    return jnp.dot(a, b, preferred_element_type=f32)


def place():
    dp = lax.axis_index("dp")
    seq = lax.axis_index("seq")
    return dp, lax.div(seq, 4), lax.rem(seq, 4)


def plane_barrier(dp, y, z):
    barrier = pltpu.get_barrier_semaphore()
    for r in (1, 2, 3):
        for seq in (lax.rem(y + r, 4) * 4 + z, y * 4 + lax.rem(z + r, 4)):
            pl.semaphore_signal(barrier, inc=1, device_id={"seq": seq}, device_id_type=MESH)
    pl.semaphore_signal(barrier, inc=1, device_id={"dp": 1 - dp}, device_id_type=MESH)
    pl.semaphore_wait(barrier, 7)


def tensor_barrier(ti):
    barrier = pltpu.get_barrier_semaphore()
    for r in (1, 2, 3):
        pl.semaphore_signal(
            barrier, inc=1, device_id={"tensor": lax.rem(ti + r, 4)}, device_id_type=MESH
        )
    pl.semaphore_wait(barrier, 3)


def both_barrier(ti, si):
    barrier = pltpu.get_barrier_semaphore()
    for r in (1, 2, 3):
        pl.semaphore_signal(
            barrier, inc=1, device_id={"tensor": lax.rem(ti + r, 4)}, device_id_type=MESH
        )

    def greet(r, carry):
        pl.semaphore_signal(
            barrier, inc=1, device_id={"seq": lax.rem(si + r, 16)}, device_id_type=MESH
        )
        return carry

    lax.fori_loop(1, 16, greet, 0)
    pl.semaphore_wait(barrier, 18)


def own_rows(ti):
    return pl.ds(pl.multiple_of(ti * 64, 64), 64)


def scatter_copies(part, landing, ss, rs, base, ti):
    copies = []
    for r in (1, 2, 3):
        p = lax.rem(ti + r, 4)
        copies.append(
            remote(
                part.at[own_rows(p)],
                landing.at[r - 1],
                ss.at[base + r - 1],
                rs.at[base + r - 1],
                {"tensor": p},
            )
        )
    return copies


def gather_copies(full, ss, rs, base, ti):
    copies = []
    for r in (1, 2, 3):
        p = lax.rem(ti + r, 4)
        copies.append(
            remote(
                full.at[own_rows(ti)],
                full.at[own_rows(ti)],
                ss.at[base + r - 1],
                rs.at[base + r - 1],
                {"tensor": p},
            )
        )
    return copies


def gather_waits(full, ss, rs, base, ti):
    for r in (1, 2, 3):
        p = lax.rem(ti + 4 - r, 4)
        copy = remote(
            full.at[own_rows(p)],
            full.at[own_rows(p)],
            ss.at[base + r - 1],
            rs.at[base + r - 1],
            {"tensor": p},
        )
        copy.wait_recv()
    for r in (1, 2, 3):
        p = lax.rem(ti + r, 4)
        copy = remote(
            full.at[own_rows(ti)],
            full.at[own_rows(ti)],
            ss.at[base + r - 1],
            rs.at[base + r - 1],
            {"tensor": p},
        )
        copy.wait_send()


def start(copies):
    for copy in copies:
        copy.start()


def wait(copies):
    for copy in copies:
        copy.wait()


def gather_weights_kernel(wa, wf, oa, of, loc, ss, rs):
    dp, y, z = place()
    plane_barrier(dp, y, z)
    arrays = ((wa, oa, SPLIT_A, CA, 0), (wf, of, SPLIT_F, CF, 25))
    local = []
    for n, (own, out, cut, width, base) in enumerate(arrays):
        copy = pltpu.make_async_copy(own, out.at[dp, y, z], loc.at[n])
        copy.start()
        local.append(copy)

    def seq_id(yy, zz):
        return {"seq": lax.rem(yy, 4) * 4 + lax.rem(zz, 4)}

    sibling = {"dp": 1 - dp}

    def first(own, out, cut, width, base, r):
        a = remote(
            own.at[:, pl.ds(0, cut)],
            out.at[dp, y, z, :, pl.ds(0, cut)],
            ss.at[base + r - 1],
            rs.at[base + r - 1],
            seq_id(y + r, z),
        )
        b = remote(
            own.at[:, pl.ds(cut, width - cut)],
            out.at[dp, y, z, :, pl.ds(cut, width - cut)],
            ss.at[base + 3 + r - 1],
            rs.at[base + 3 + r - 1],
            seq_id(y, z + r),
        )
        return a, b

    def second(out, cut, width, base, r, yy, zz):
        src_a = out.at[dp, :, zz, :, pl.ds(0, cut)]
        src_b = out.at[dp, yy, :, :, pl.ds(cut, width - cut)]
        a = remote(
            src_a, src_a, ss.at[base + 6 + r - 1], rs.at[base + 6 + r - 1], seq_id(y, z + r)
        )
        b = remote(
            src_b, src_b, ss.at[base + 9 + r - 1], rs.at[base + 9 + r - 1], seq_id(y + r, z)
        )
        return a, b

    started = []
    for own, out, cut, width, base in arrays:
        for r in (1, 3, 2):
            for copy in first(own, out, cut, width, base, r):
                copy.start()
                started.append(copy)

    def to_sibling(ref, base, k):
        copy = remote(ref, ref, ss.at[base + k], rs.at[base + k], sibling)
        copy.start()
        started.append(copy)

    for copy in local:
        copy.wait()
    for own, out, cut, width, base in arrays:
        to_sibling(out.at[dp, y, z], base, 12)
        for r in (1, 3, 2):
            yy, zz = lax.rem(y + 4 - r, 4), lax.rem(z + 4 - r, 4)
            ref_a = out.at[dp, yy, z, :, pl.ds(0, cut)]
            ref_b = out.at[dp, y, zz, :, pl.ds(cut, width - cut)]
            remote(
                ref_a, ref_a, ss.at[base + r - 1], rs.at[base + r - 1], seq_id(y, z)
            ).wait_recv()
            remote(
                ref_b, ref_b, ss.at[base + 3 + r - 1], rs.at[base + 3 + r - 1], seq_id(y, z)
            ).wait_recv()
            to_sibling(ref_a, base, 13 + r - 1)
            to_sibling(ref_b, base, 16 + r - 1)
        for r in (1, 3, 2):
            for copy in second(out, cut, width, base, r, y, z):
                copy.start()
                started.append(copy)
    for own, out, cut, width, base in arrays:
        for r in (1, 3, 2):
            yy, zz = lax.rem(y + 4 - r, 4), lax.rem(z + 4 - r, 4)
            ref_a = out.at[dp, :, zz, :, pl.ds(0, cut)]
            ref_b = out.at[dp, yy, :, :, pl.ds(cut, width - cut)]
            remote(
                ref_a, ref_a, ss.at[base + 6 + r - 1], rs.at[base + 6 + r - 1], seq_id(y, z)
            ).wait_recv()
            to_sibling(ref_a, base, 19 + r - 1)
            remote(
                ref_b, ref_b, ss.at[base + 9 + r - 1], rs.at[base + 9 + r - 1], seq_id(y, z)
            ).wait_recv()
            to_sibling(ref_b, base, 22 + r - 1)
    other = 1 - dp
    for own, out, cut, width, base in arrays:
        refs = [(12, out.at[other, y, z])]
        for r in (1, 3, 2):
            yy, zz = lax.rem(y + 4 - r, 4), lax.rem(z + 4 - r, 4)
            refs.append((13 + r - 1, out.at[other, yy, z, :, pl.ds(0, cut)]))
            refs.append((16 + r - 1, out.at[other, y, zz, :, pl.ds(cut, width - cut)]))
            refs.append((19 + r - 1, out.at[other, :, zz, :, pl.ds(0, cut)]))
            refs.append((22 + r - 1, out.at[other, yy, :, :, pl.ds(cut, width - cut)]))
        for k, ref in refs:
            remote(ref, ref, ss.at[base + k], rs.at[base + k], sibling).wait_recv()
    for copy in started:
        copy.wait_send()


def gather_weights(wa, wf):
    return pl.pallas_call(
        gather_weights_kernel,
        out_shape=(
            jax.ShapeDtypeStruct((2, 4, 4, 32, CA), bf16),
            jax.ShapeDtypeStruct((2, 4, 4, 32, CF), bf16),
        ),
        in_specs=[VMEM, VMEM],
        out_specs=(ANY, ANY),
        scratch_shapes=[
            pltpu.SemaphoreType.DMA((2,)),
            pltpu.SemaphoreType.DMA((50,)),
            pltpu.SemaphoreType.DMA((50,)),
        ],
        compiler_params=params(1),
        name="gather_weights",
    )(wa, wf)


def head_stack(pieces):
    zero = jnp.zeros((HD, 512), pieces.dtype)
    low = jnp.concatenate([pieces[0:64], pieces[64:128]], axis=1)
    high = jnp.concatenate([pieces[128:192], pieces[192:256]], axis=1)
    top = jnp.concatenate([low, zero], axis=1)
    bottom = jnp.concatenate([zero, high], axis=1)
    return jnp.concatenate([top, bottom], axis=0)


def causal_block():
    keys = lax.broadcasted_iota(jnp.int32, (ROWS, 1024), 0)
    rows = lax.broadcasted_iota(jnp.int32, (ROWS, 1024), 1)
    return keys <= jnp.bitwise_and(rows, ROWS - 1)


def attention_forward_kernel(
    x, wa, hg, cs, h1, qkt, qpad, kv, o16, lse, h2, hres, gains, acc, part, landing, ss, rs, ts, tr
):
    si = lax.axis_index("seq")
    ti = lax.axis_index("tensor")
    both_barrier(ti, si)
    gains[...] = wa[:, 768:896].astype(f32).T[0:8]
    x32 = x[...].astype(f32)
    inverse = lax.rsqrt(jnp.mean(x32 * x32, axis=-1, keepdims=True) + norm_eps)
    h1[...] = (x32 * inverse * gains[0:1]).astype(bf16)
    qkv = dot_nn(h1[...], wa[:, 0:512])
    qk = qkv[:, 0:384].T
    qkt[...] = qk
    cosine, sine = cs[0:32], cs[32:64]
    rotated = []
    for h in range(6):
        one = qk[64 * h : 64 * h + 64]
        hat = one * lax.rsqrt(jnp.mean(one * one, axis=0, keepdims=True) + norm_eps)
        scaled = hat * hg[:, (0 if h < 4 else 1) : (1 if h < 4 else 2)]
        a, b = scaled[0:32], scaled[32:64]
        rotated += [a * cosine - b * sine, b * cosine + a * sine]
    q_all = jnp.concatenate(rotated[0:8], axis=0)
    k_all = jnp.concatenate(rotated[8:12], axis=0)
    kv[si, :, 0:128] = k_all.T.astype(bf16)
    kv[si, :, 128:256] = qkv[:, 384:512].astype(bf16)

    def send(r):
        return remote(kv.at[si], kv.at[si], ss.at[r], rs.at[r], {"seq": si + r})

    def send_one(r, carry):
        send(r).start()
        return carry

    lax.fori_loop(1, 16 - si, send_one, 0)
    qpad[...] = head_stack(q_all.astype(bf16))
    ones = jnp.ones((16, ROWS), bf16)

    def visit(block, diagonal):
        k16 = kv[block, :, 0:128]
        scores = dot_nn(k16, qpad[...])
        p = jnp.exp2(scores * (SCALE * LOG2E))
        if diagonal:
            p = jnp.where(causal_block(), p, 0.0)
        p16 = p.astype(bf16)
        vt = transposed(kv[block, :, 128:256], bf16)
        for j in range(2):
            lhs = jnp.concatenate([vt[64 * j : 64 * j + 64], ones], axis=0)
            out = dot_nn(lhs, p16[:, 512 * j : 512 * j + 512])
            if diagonal:
                acc[j] = out
            else:
                acc[j] += out

    visit(si, True)

    def later(r, carry):
        block = si - r
        remote(kv.at[block], kv.at[block], ss.at[r], rs.at[r], {"seq": block}).wait_recv()
        visit(block, False)
        return carry

    lax.fori_loop(1, si + 1, later, 0)
    pieces = []
    for j in range(2):
        total = acc[j, 64:65]
        out = acc[j, 0:64] / total
        lse[j : j + 1] = jnp.log(total) * LOG2E
        pieces += [out[:, 0:256], out[:, 256:512]]
    o16[...] = jnp.concatenate(pieces, axis=0).T.astype(bf16)
    part[...] = dot_nt(o16[...], wa[:, 512:768]).astype(bf16)
    copies = scatter_copies(part, landing, ts, tr, 0, ti)
    start(copies)
    wait(copies)
    rows = own_rows(ti)
    total = x[rows].astype(f32) + part[rows].astype(f32)
    for r in range(3):
        total += landing[r].astype(f32)
    hres[...] = total
    inverse = lax.rsqrt(jnp.mean(total * total, axis=-1, keepdims=True) + norm_eps)
    h2[rows] = (total * inverse * gains[1:2]).astype(bf16)
    start(gather_copies(h2, ts, tr, 3, ti))

    def send_done(r, carry):
        send(r).wait_send()
        return carry

    lax.fori_loop(1, 16 - si, send_done, 0)
    gather_waits(h2, ts, tr, 3, ti)


def attention_forward(x, wa, hg, cs):
    return pl.pallas_call(
        attention_forward_kernel,
        out_shape=(
            jax.ShapeDtypeStruct((256, 1024), bf16),
            jax.ShapeDtypeStruct((384, 256), f32),
            jax.ShapeDtypeStruct((128, 1024), bf16),
            jax.ShapeDtypeStruct((16, 256, 256), bf16),
            jax.ShapeDtypeStruct((256, 256), bf16),
            jax.ShapeDtypeStruct((2, 512), f32),
            jax.ShapeDtypeStruct((256, 1024), bf16),
            jax.ShapeDtypeStruct((64, 1024), f32),
            jax.ShapeDtypeStruct((8, 1024), f32),
        ),
        in_specs=[VMEM] * 4,
        out_specs=(VMEM,) * 9,
        scratch_shapes=[
            pltpu.VMEM((2, 80, 512), f32),
            pltpu.VMEM((256, 1024), bf16),
            pltpu.VMEM((3, 64, 1024), bf16),
            pltpu.SemaphoreType.DMA((16,)),
            pltpu.SemaphoreType.DMA((16,)),
            pltpu.SemaphoreType.DMA((6,)),
            pltpu.SemaphoreType.DMA((6,)),
        ],
        compiler_params=params(2),
        name="attention_forward",
    )(x, wa, hg, cs)


def feed_forward_kernel(
    h2, dy, wf, hres, gains, out, dres16, dres, gf, n2sum,
    z, dg, du, po, pd, lo, ld, dyt, h2t, ts, tr,
):
    ti = lax.axis_index("tensor")
    tensor_barrier(ti)
    width = 384

    def hidden(c, carry):
        at = pl.multiple_of(c * width, 128)
        gate = dot_nn(h2[...], wf[:, pl.ds(at, width)])
        up = dot_nn(h2[...], wf[:, pl.ds(at + FFC, width)])
        dz = dot_nn(dy[...], wf[:, pl.ds(at + 2 * FFC, width)])
        sigma = jax.nn.sigmoid(gate)
        silu = gate * sigma
        z[:, pl.ds(at, width)] = (silu * up).astype(bf16)
        dg[:, pl.ds(at, width)] = (dz * up * sigma * (1.0 + gate * (1.0 - sigma))).astype(bf16)
        du[:, pl.ds(at, width)] = (dz * silu).astype(bf16)
        return carry

    lax.fori_loop(0, 3, hidden, 0)

    def back(n, carry):
        at = pl.ds(pl.multiple_of(n * 256, 256), 256)
        pd[:, at] = (
            dot_nt(dg[...], wf[at, 0:FFC]) + dot_nt(du[...], wf[at, FFC : 2 * FFC])
        ).astype(bf16)
        po[:, at] = dot_nt(z[...], wf[at, 2 * FFC : 3 * FFC]).astype(bf16)
        return carry

    lax.fori_loop(0, 4, back, 0)
    copies_d = scatter_copies(pd, ld, ts, tr, 0, ti)
    copies_o = scatter_copies(po, lo, ts, tr, 3, ti)
    start(copies_d)
    start(copies_o)
    h2t[...] = transposed(h2[...], bf16)
    dyt[...] = transposed(dy[...], bf16)

    def gate_grads(n, carry):
        at = pl.ds(pl.multiple_of(n * 256, 256), 256)
        gf[at, 0:FFC] = dot_nn(h2t[at], dg[...]).astype(bf16)
        gf[at, FFC : 2 * FFC] = dot_nn(h2t[at], du[...]).astype(bf16)
        return carry

    lax.fori_loop(0, 4, gate_grads, 0)
    wait(copies_d)
    wait(copies_o)
    rows = own_rows(ti)
    dh2 = pd[rows].astype(f32)
    ffn = po[rows].astype(f32)
    for r in range(3):
        dh2 += ld[r].astype(f32)
        ffn += lo[r].astype(f32)
    mid = hres[...]
    out[rows] = (mid + ffn).astype(bf16)
    inverse = lax.rsqrt(jnp.mean(mid * mid, axis=-1, keepdims=True) + norm_eps)
    normed = mid * inverse
    scaled = dh2 * gains[1:2]
    inner = jnp.mean(scaled * normed, axis=-1, keepdims=True)
    grad = dy[rows].astype(f32) + inverse * (scaled - normed * inner)
    dres[...] = grad
    dres16[rows] = grad.astype(bf16)
    start(gather_copies(dres16, ts, tr, 6, ti))
    start(gather_copies(out, ts, tr, 9, ti))
    n2sum[...] = jnp.broadcast_to(jnp.sum(dh2 * normed, axis=0, keepdims=True), (8, 1024))

    def down_grads(n, carry):
        at = pl.ds(pl.multiple_of(n * 256, 256), 256)
        gf[at, 2 * FFC : 3 * FFC] = dot_nn(dyt[at], z[...]).astype(bf16)
        return carry

    lax.fori_loop(0, 4, down_grads, 0)
    gather_waits(dres16, ts, tr, 6, ti)
    gather_waits(out, ts, tr, 9, ti)


def feed_forward(h2, dy, wf, hres, gains):
    return pl.pallas_call(
        feed_forward_kernel,
        out_shape=(
            jax.ShapeDtypeStruct((256, 1024), bf16),
            jax.ShapeDtypeStruct((256, 1024), bf16),
            jax.ShapeDtypeStruct((64, 1024), f32),
            jax.ShapeDtypeStruct((1024, CF), bf16),
            jax.ShapeDtypeStruct((8, 1024), f32),
        ),
        in_specs=[VMEM] * 5,
        out_specs=(VMEM,) * 5,
        scratch_shapes=[
            pltpu.VMEM((256, FFC), bf16),
            pltpu.VMEM((256, FFC), bf16),
            pltpu.VMEM((256, FFC), bf16),
            pltpu.VMEM((256, 1024), bf16),
            pltpu.VMEM((256, 1024), bf16),
            pltpu.VMEM((3, 64, 1024), bf16),
            pltpu.VMEM((3, 64, 1024), bf16),
            pltpu.VMEM((1024, 256), bf16),
            pltpu.VMEM((1024, 256), bf16),
            pltpu.SemaphoreType.DMA((12,)),
            pltpu.SemaphoreType.DMA((12,)),
        ],
        compiler_params=params(3),
        name="feed_forward",
    )(h2, dy, wf, hres, gains)


def attention_backward_kernel(
    x, wa, hg, cs, h1, qkt, qpad, kv, o16, lse, gains, dres16, dres, n2sum,
    ga, input_grad, heads,
    dot_pad, do_nat, q_nat, delta, dq, dkv, dkv_in, part, landing, ig16, small, ss, rs, ts, tr,
):
    si = lax.axis_index("seq")
    ti = lax.axis_index("tensor")
    both_barrier(ti, si)
    do_t = transposed(dot_nn(dres16[...], wa[:, 512:768]).astype(bf16), f32)
    o_t = transposed(o16[...], f32)
    products = do_t * o_t
    sums = [jnp.sum(products[64 * h : 64 * h + 64], axis=0, keepdims=True) for h in range(4)]
    delta[...] = jnp.concatenate(sums, axis=1)
    dot_pad[...] = head_stack(do_t.astype(bf16))
    do_nat[...] = transposed(dot_pad[...], bf16)
    q_nat[...] = transposed(qpad[...], bf16)

    def visit(block, diagonal):
        k16 = kv[block, :, 0:128]
        kt = transposed(k16, bf16)
        scores = dot_nn(k16, qpad[...])
        shift = jnp.concatenate([lse[0:1], lse[1:2]], axis=1)
        p = jnp.exp2(scores * (SCALE * LOG2E) - shift)
        if diagonal:
            p = jnp.where(causal_block(), p, 0.0)
        dp = dot_nn(kv[block, :, 128:256], dot_pad[...])
        ds16 = (p * (dp - delta[...])).astype(bf16)
        dkv[block, :, 0:128] = (dot_nn(ds16, q_nat[...]) * SCALE).astype(bf16)
        dkv[block, :, 128:256] = dot_nn(p.astype(bf16), do_nat[...]).astype(bf16)
        for j in range(2):
            out = dot_nn(kt[64 * j : 64 * j + 64], ds16[:, 512 * j : 512 * j + 512])
            if diagonal:
                dq[j] = out
            else:
                dq[j] += out

    visit(si, True)

    def send(r):
        return remote(dkv.at[si - r], dkv_in.at[r], ss.at[r], rs.at[r], {"seq": si - r})

    def later(r, carry):
        visit(si - r, False)
        send(r).start()
        return carry

    lax.fori_loop(1, si + 1, later, 0)

    hats, inverses = [], []
    for h in range(6):
        one = qkt[64 * h : 64 * h + 64]
        inverse = lax.rsqrt(jnp.mean(one * one, axis=0, keepdims=True) + norm_eps)
        inverses.append(inverse)
        hats.append(one * inverse)
    cosine, sine = cs[0:32], cs[32:64]

    def head_back(gradient, h):
        a, b = gradient[0:32], gradient[32:64]
        normed = jnp.concatenate([a * cosine + b * sine, b * cosine - a * sine], axis=0)
        gain = hg[:, 0:1] if h < 4 else hg[:, 1:2]
        scaled = normed * gain
        inner = jnp.mean(scaled * hats[h], axis=0, keepdims=True)
        return inverses[h] * (scaled - hats[h] * inner), normed * hats[h]

    results, q_products = [], 0.0
    for h in range(4):
        piece = dq[h // 2, :, 256 * (h % 2) : 256 * (h % 2) + 256] * SCALE
        result, product = head_back(piece, h)
        results.append(result)
        q_products = q_products + product
    ga[:, 512:768] = dot_nn(transposed(dres16[...], bf16), o16[...]).astype(bf16)

    def receive(r, total):
        remote(dkv.at[si], dkv_in.at[r], ss.at[r], rs.at[r], {"seq": si}).wait_recv()
        return total + dkv_in[r].astype(f32)

    total = lax.fori_loop(1, 16 - si, receive, dkv[si].astype(f32))
    dkt = total[:, 0:128].T
    k_products = 0.0
    for h in range(2):
        result, product = head_back(dkt[64 * h : 64 * h + 64], 4 + h)
        results.append(result)
        k_products = k_products + product
    dqk = jnp.concatenate(results, axis=0).T.astype(bf16)
    dqkv = jnp.concatenate([dqk, total[:, 128:256].astype(bf16)], axis=1)
    part[...] = dot_nt(dqkv, wa[:, 0:512]).astype(bf16)
    copies = scatter_copies(part, landing, ts, tr, 0, ti)
    start(copies)
    ga[:, 0:512] = dot_nn(transposed(h1[...], bf16), dqkv).astype(bf16)
    head_rows = jnp.concatenate(
        [
            jnp.sum(q_products.T, axis=0, keepdims=True),
            jnp.sum(k_products.T, axis=0, keepdims=True),
            jnp.zeros((1, 896), f32),
        ],
        axis=1,
    )
    wait(copies)
    rows = own_rows(ti)
    dh1 = part[rows].astype(f32)
    for r in range(3):
        dh1 += landing[r].astype(f32)
    x32 = x[rows].astype(f32)
    inverse = lax.rsqrt(jnp.mean(x32 * x32, axis=-1, keepdims=True) + norm_eps)
    normed = x32 * inverse
    scaled = dh1 * gains[0:1]
    inner = jnp.mean(scaled * normed, axis=-1, keepdims=True)
    ig16[rows] = (dres[...] + inverse * (scaled - normed * inner)).astype(bf16)
    start(gather_copies(ig16, ts, tr, 3, ti))
    small[0] = jnp.concatenate(
        [
            jnp.sum(dh1 * normed, axis=0, keepdims=True),
            n2sum[0:1],
            head_rows,
            jnp.zeros((5, 1024), f32),
        ],
        axis=0,
    )

    def small_copy(r):
        return remote(
            small.at[0], small.at[r], ts.at[6 + r - 1], tr.at[6 + r - 1], {"tensor": lax.rem(ti + r, 4)}
        )

    copies = [small_copy(r) for r in (1, 2, 3)]
    start(copies)
    wait(copies)
    sums = small[0] + small[1] + small[2] + small[3]
    ga[:, 768:896] = jnp.concatenate([sums, jnp.zeros((120, 1024), f32)], axis=0).T.astype(bf16)
    heads[...] = jnp.broadcast_to(sums[2:3, 0:128], (8, 128))

    def send_done(r, carry):
        send(r).wait_send()
        return carry

    lax.fori_loop(1, si + 1, send_done, 0)
    gather_waits(ig16, ts, tr, 3, ti)
    input_grad[...] = ig16[...].astype(f32)


def attention_backward(*operands):
    return pl.pallas_call(
        attention_backward_kernel,
        out_shape=(
            jax.ShapeDtypeStruct((1024, CA), bf16),
            jax.ShapeDtypeStruct((256, 1024), f32),
            jax.ShapeDtypeStruct((8, 128), f32),
        ),
        in_specs=[VMEM] * 14,
        out_specs=(VMEM,) * 3,
        scratch_shapes=[
            pltpu.VMEM((128, 1024), bf16),
            pltpu.VMEM((1024, 128), bf16),
            pltpu.VMEM((1024, 128), bf16),
            pltpu.VMEM((1, 1024), f32),
            pltpu.VMEM((2, 64, 512), f32),
            pltpu.VMEM((16, 256, 256), bf16),
            pltpu.VMEM((16, 256, 256), bf16),
            pltpu.VMEM((256, 1024), bf16),
            pltpu.VMEM((3, 64, 1024), bf16),
            pltpu.VMEM((256, 1024), bf16),
            pltpu.VMEM((4, 8, 1024), f32),
            pltpu.SemaphoreType.DMA((16,)),
            pltpu.SemaphoreType.DMA((16,)),
            pltpu.SemaphoreType.DMA((9,)),
            pltpu.SemaphoreType.DMA((9,)),
        ],
        compiler_params=params(4),
        name="attention_backward",
    )(*operands)


def scatter_gradients_kernel(
    ga, gf, heads, fa, ff, hsum,
    sa, sf, ra, rf, wa1, wb1, wf1, xf1, ta, tb, tf, uf, va, vb, vf, yf, hs, hr, ss, rs, hss, hrs,
):
    dp, y, z = place()
    plane_barrier(dp, y, z)
    sibling = {"dp": 1 - dp}

    def seq_id(yy, zz):
        return {"seq": lax.rem(yy, 4) * 4 + lax.rem(zz, 4)}

    arrays = (
        (gf, rf, sf, SPLIT_F, CF, 13, (wf1, tf, vf), (xf1, uf, yf), ff),
        (ga, ra, sa, SPLIT_A, CA, 0, (wa1, ta, va), (wb1, tb, vb), fa),
    )
    started = []
    head_copy = remote(heads, hr.at[0], hss.at[0], hrs.at[0], sibling)
    head_copy.start()
    pair = []
    for g, landing, total, cut, width, base, _, _, _ in arrays:
        copy = remote(g.at[1 - dp], landing, ss.at[base + 12], rs.at[base + 12], sibling)
        copy.start()
        pair.append(copy)
    head_copy.wait()
    hs[0] = heads[...] + hr[0]
    head_z = [
        remote(hs.at[0], hr.at[r], hss.at[r], hrs.at[r], seq_id(y, z + r)) for r in (1, 2, 3)
    ]
    start(head_z)
    for n, (g, landing, total, cut, width, base, half_a, half_b, _) in enumerate(arrays):
        pair[n].wait()

        def add(i, carry):
            yy, zz = lax.div(i, 4), lax.rem(i, 4)
            total[yy, zz] = (
                g[dp, yy, zz].astype(f32) + landing[yy, zz].astype(f32)
            ).astype(bf16)
            return carry

        lax.fori_loop(0, 16, add, 0)
        for r in (2, 1, 3):
            zz, yy = lax.rem(z + r, 4), lax.rem(y + r, 4)
            a = remote(
                total.at[:, zz, :, pl.ds(0, cut)],
                half_a[0].at[r - 1],
                ss.at[base + r - 1],
                rs.at[base + r - 1],
                seq_id(y, z + r),
            )
            b = remote(
                total.at[yy, :, :, pl.ds(cut, width - cut)],
                half_b[0].at[r - 1],
                ss.at[base + 3 + r - 1],
                rs.at[base + 3 + r - 1],
                seq_id(y + r, z),
            )
            a.start()
            b.start()
            started.append((n, 0, a))
            started.append((n, 1, b))
    for copy in head_z:
        copy.wait()
    hs[1] = hs[0] + hr[1] + hr[2] + hr[3]
    head_y = [
        remote(hs.at[1], hr.at[3 + r], hss.at[3 + r], hrs.at[3 + r], seq_id(y + r, z))
        for r in (1, 2, 3)
    ]
    start(head_y)
    final = []
    for n, (g, landing, total, cut, width, base, half_a, half_b, _) in enumerate(arrays):
        for m, half in ((0, half_a), (1, half_b)):
            for k, which, copy in started:
                if (k, which) == (n, m):
                    copy.wait()

            def add(i, carry):
                if m == 0:
                    mine = total[i, z, :, 0:cut]
                else:
                    mine = total[y, i, :, cut:width]
                summed = mine.astype(f32)
                for r in range(3):
                    summed += half[0][r, i].astype(f32)
                half[1][i] = summed.astype(bf16)
                return carry

            lax.fori_loop(0, 4, add, 0)
            for r in (2, 1, 3):
                if m == 0:
                    to, target = lax.rem(y + r, 4), seq_id(y + r, z)
                else:
                    to, target = lax.rem(z + r, 4), seq_id(y, z + r)
                k = base + 6 + 3 * m + r - 1
                copy = remote(half[1].at[to], half[2].at[r - 1], ss.at[k], rs.at[k], target)
                copy.start()
                final.append((n, m, copy))
    for copy in head_y:
        copy.wait()
    hsum[...] = hs[1] + hr[4] + hr[5] + hr[6]
    for n, (g, landing, total, cut, width, base, half_a, half_b, result) in enumerate(arrays):
        for m, half in ((0, half_a), (1, half_b)):
            for k, which, copy in final:
                if (k, which) == (n, m):
                    copy.wait()
            mine = y if m == 0 else z
            summed = half[1][mine].astype(f32)
            for r in range(3):
                summed += half[2][r].astype(f32)
            if m == 0:
                result[:, 0:cut] = summed
            else:
                result[:, cut:width] = summed


def scatter_gradients(ga, gf, heads):
    def block(*shape):
        return pltpu.VMEM(shape, bf16)

    rest_a, rest_f = CA - SPLIT_A, CF - SPLIT_F
    return pl.pallas_call(
        scatter_gradients_kernel,
        out_shape=(
            jax.ShapeDtypeStruct((32, CA), f32),
            jax.ShapeDtypeStruct((32, CF), f32),
            jax.ShapeDtypeStruct((8, 128), f32),
        ),
        in_specs=[VMEM] * 3,
        out_specs=(VMEM,) * 3,
        scratch_shapes=[
            block(4, 4, 32, CA),
            block(4, 4, 32, CF),
            block(4, 4, 32, CA),
            block(4, 4, 32, CF),
            block(3, 4, 32, SPLIT_A),
            block(3, 4, 32, rest_a),
            block(3, 4, 32, SPLIT_F),
            block(3, 4, 32, rest_f),
            block(4, 32, SPLIT_A),
            block(4, 32, rest_a),
            block(4, 32, SPLIT_F),
            block(4, 32, rest_f),
            block(3, 32, SPLIT_A),
            block(3, 32, rest_a),
            block(3, 32, SPLIT_F),
            block(3, 32, rest_f),
            pltpu.VMEM((2, 8, 128), f32),
            pltpu.VMEM((7, 8, 128), f32),
            pltpu.SemaphoreType.DMA((26,)),
            pltpu.SemaphoreType.DMA((26,)),
            pltpu.SemaphoreType.DMA((7,)),
            pltpu.SemaphoreType.DMA((7,)),
        ],
        compiler_params=params(5),
        name="scatter_gradients",
    )(ga.reshape(2, 4, 4, 32, CA), gf.reshape(2, 4, 4, 32, CF), heads)


def adamw(weight, momentum, variance, gradient, decay):
    first = beta_one * momentum + (1.0 - beta_one) * gradient
    second = beta_two * variance + (1.0 - beta_two) * gradient * gradient
    first_fixed = first / (1.0 - beta_one**adam_count)
    second_fixed = second / (1.0 - beta_two**adam_count)
    direction = first_fixed / (jnp.sqrt(second_fixed) + adam_eps) + decay * weight
    return (direction, first, second)


def body(
    block_input,
    upstream_grad,
    query_weight,
    key_value_weight,
    output_weight,
    gateup_weight,
    down_weight,
    norm_gains,
    head_norm_gains,
    query_momentum,
    query_variance,
    key_value_momentum,
    key_value_variance,
    output_momentum,
    output_variance,
    gateup_momentum,
    gateup_variance,
    down_momentum,
    down_variance,
    norm_momentum,
    norm_variance,
    head_momentum,
    head_variance,
):
    x = block_input[0]
    dy = upstream_grad[0]
    wa_own = jnp.concatenate(
        [
            query_weight,
            key_value_weight[:, 0],
            key_value_weight[:, 1],
            output_weight,
            jnp.pad(norm_gains, ((0, 0), (0, 126))),
        ],
        axis=1,
    ).astype(bf16)
    wf_own = jnp.concatenate(
        [gateup_weight[:, 0], gateup_weight[:, 1], down_weight], axis=1
    ).astype(bf16)
    wa, wf = gather_weights(wa_own, wf_own)
    wa = wa.reshape(1024, CA)
    wf = wf.reshape(1024, CF)
    positions = lax.axis_index("seq") * ROWS + jnp.arange(ROWS, dtype=jnp.int32)
    frequency = rope_base ** (-(jnp.arange(HD // 2, dtype=f32) * 2.0) / HD)
    angles = positions.astype(f32)[None, :] * frequency[:, None]
    cs = jnp.concatenate([jnp.cos(angles), jnp.sin(angles)], axis=0)
    hg = head_norm_gains.T
    h1, qkt, qpad, kv, o16, lse, h2, hres, gains = attention_forward(x, wa, hg, cs)
    out, dres16, dres, gf, n2sum = feed_forward(h2, dy, wf, hres, gains)
    ga, input_grad, heads = attention_backward(
        x, wa, hg, cs, h1, qkt, qpad, kv, o16, lse, gains, dres16, dres, n2sum
    )
    fa, ff, hsum = scatter_gradients(ga, gf, heads)
    grad_q = fa[:, 0:256]
    grad_kv = jnp.stack([fa[:, 256:384], fa[:, 384:512]], axis=1)
    grad_o = fa[:, 512:768]
    grad_n = fa[:, 768:770]
    grad_gu = jnp.stack([ff[:, 0:FFC], ff[:, FFC : 2 * FFC]], axis=1)
    grad_d = ff[:, 2 * FFC :]
    head_grad = jnp.stack([hsum[0, 0:64], hsum[0, 64:128]], axis=0)
    new_q = adamw(query_weight, query_momentum, query_variance, grad_q, decay_rate)
    new_kv = adamw(key_value_weight, key_value_momentum, key_value_variance, grad_kv, decay_rate)
    new_o = adamw(output_weight, output_momentum, output_variance, grad_o, decay_rate)
    new_gu = adamw(gateup_weight, gateup_momentum, gateup_variance, grad_gu, decay_rate)
    new_d = adamw(down_weight, down_momentum, down_variance, grad_d, decay_rate)
    new_n = adamw(norm_gains, norm_momentum, norm_variance, grad_n, 0.0)
    new_h = adamw(head_norm_gains, head_momentum, head_variance, head_grad, 0.0)
    return (
        out[None],
        input_grad[None],
        grad_q,
        grad_kv,
        grad_o,
        grad_gu,
        grad_d,
        grad_n,
        head_grad,
        new_q[0],
        new_kv[0],
        new_o[0],
        new_gu[0],
        new_d[0],
        new_n[0],
        new_h[0],
        new_q[1],
        new_q[2],
        new_kv[1],
        new_kv[2],
        new_o[1],
        new_o[2],
        new_gu[1],
        new_gu[2],
        new_d[1],
        new_d[2],
        new_n[1],
        new_n[2],
        new_h[1],
        new_h[2],
    )


def solution(mesh):
    in_specs = (
        P("dp", "seq", None),
        P("dp", "seq", None),
        P(("dp", "seq"), "tensor"),
        P(("dp", "seq"), None, "tensor"),
        P(("dp", "seq"), "tensor"),
        P(("dp", "seq"), None, "tensor"),
        P(("dp", "seq"), "tensor"),
        P(("dp", "seq"), None),
        P(),
        P(("dp", "seq"), "tensor"),
        P(("dp", "seq"), "tensor"),
        P(("dp", "seq"), None, "tensor"),
        P(("dp", "seq"), None, "tensor"),
        P(("dp", "seq"), "tensor"),
        P(("dp", "seq"), "tensor"),
        P(("dp", "seq"), None, "tensor"),
        P(("dp", "seq"), None, "tensor"),
        P(("dp", "seq"), "tensor"),
        P(("dp", "seq"), "tensor"),
        P(("dp", "seq"), None),
        P(("dp", "seq"), None),
        P(),
        P(),
    )
    out_specs = (
        P("dp", "seq", None),
        P("dp", "seq", None),
        P(("dp", "seq"), "tensor"),
        P(("dp", "seq"), None, "tensor"),
        P(("dp", "seq"), "tensor"),
        P(("dp", "seq"), None, "tensor"),
        P(("dp", "seq"), "tensor"),
        P(("dp", "seq"), None),
        P(),
        P(("dp", "seq"), "tensor"),
        P(("dp", "seq"), None, "tensor"),
        P(("dp", "seq"), "tensor"),
        P(("dp", "seq"), None, "tensor"),
        P(("dp", "seq"), "tensor"),
        P(("dp", "seq"), None),
        P(),
        P(("dp", "seq"), "tensor"),
        P(("dp", "seq"), "tensor"),
        P(("dp", "seq"), None, "tensor"),
        P(("dp", "seq"), None, "tensor"),
        P(("dp", "seq"), "tensor"),
        P(("dp", "seq"), "tensor"),
        P(("dp", "seq"), None, "tensor"),
        P(("dp", "seq"), None, "tensor"),
        P(("dp", "seq"), "tensor"),
        P(("dp", "seq"), "tensor"),
        P(("dp", "seq"), None),
        P(("dp", "seq"), None),
        P(),
        P(),
    )
    return jax.shard_map(body, mesh=mesh, in_specs=in_specs, out_specs=out_specs, check_vma=False)
```

```python
import numpy as np
import jax
import jax.numpy as jnp
from jax import lax
from jax.experimental import pallas as pl
from jax.experimental.pallas import tpu as pltpu
from jax.sharding import PartitionSpec as P

f32 = jnp.float32
bf16 = jnp.bfloat16
MESH = pl.DeviceIdType.MESH
norm_eps = 1e-05
rope_base = 1000000.0
beta_one = 0.9
beta_two = 0.95
adam_eps = 1e-08
decay_rate = 0.1
adam_count = 3
LOG2E = 1.4426950408889634
ROWS = 256
HD = 64
SCALE = 0.125
CA = 896
CG = 768
CF = 3456
FFC = 1152
SPLIT_A = 512
SPLIT_G = 384
SPLIT_F = 1792
VMEM = pl.BlockSpec(memory_space=pltpu.VMEM)
ANY = pl.BlockSpec(memory_space=pl.ANY)


def params(collective_id, megabytes=56):
    return pltpu.CompilerParams(
        collective_id=collective_id,
        has_side_effects=True,
        vmem_limit_bytes=megabytes * 1024 * 1024,
    )


def remote(src, dst, send_sem, recv_sem, device):
    return pltpu.make_async_remote_copy(
        src_ref=src,
        dst_ref=dst,
        send_sem=send_sem,
        recv_sem=recv_sem,
        device_id=device,
        device_id_type=MESH,
    )


def transposed(x, dtype):
    return x.astype(f32).T.astype(dtype)


def dot_nt(a, b):
    return lax.dot_general(a, b, (((1,), (1,)), ((), ())), preferred_element_type=f32)


def dot_nn(a, b):
    return jnp.dot(a, b, preferred_element_type=f32)


def place():
    dp = lax.axis_index("dp")
    seq = lax.axis_index("seq")
    return dp, lax.div(seq, 4), lax.rem(seq, 4)


def own_rows(ti):
    return pl.ds(pl.multiple_of(ti * 64, 64), 64)


def scatter_copies(part, landing, ss, rs, base, ti):
    copies = []
    for r in (1, 2, 3):
        p = lax.rem(ti + r, 4)
        copies.append(
            remote(
                part.at[own_rows(p)],
                landing.at[r - 1],
                ss.at[base + r - 1],
                rs.at[base + r - 1],
                {"tensor": p},
            )
        )
    return copies


def gather_copies(full, ss, rs, base, ti):
    copies = []
    for r in (1, 2, 3):
        p = lax.rem(ti + r, 4)
        copies.append(
            remote(
                full.at[own_rows(ti)],
                full.at[own_rows(ti)],
                ss.at[base + r - 1],
                rs.at[base + r - 1],
                {"tensor": p},
            )
        )
    return copies


def gather_waits(full, ss, rs, base, ti):
    for r in (1, 2, 3):
        p = lax.rem(ti + 4 - r, 4)
        copy = remote(
            full.at[own_rows(p)],
            full.at[own_rows(p)],
            ss.at[base + r - 1],
            rs.at[base + r - 1],
            {"tensor": p},
        )
        copy.wait_recv()
    for r in (1, 2, 3):
        p = lax.rem(ti + r, 4)
        copy = remote(
            full.at[own_rows(ti)],
            full.at[own_rows(ti)],
            ss.at[base + r - 1],
            rs.at[base + r - 1],
            {"tensor": p},
        )
        copy.wait_send()


def start(copies):
    for copy in copies:
        copy.start()


def wait(copies):
    for copy in copies:
        copy.wait()


def head_stack(pieces):
    zero = jnp.zeros((HD, 512), pieces.dtype)
    low = jnp.concatenate([pieces[0:64], pieces[64:128]], axis=1)
    high = jnp.concatenate([pieces[128:192], pieces[192:256]], axis=1)
    top = jnp.concatenate([low, zero], axis=1)
    bottom = jnp.concatenate([zero, high], axis=1)
    return jnp.concatenate([top, bottom], axis=0)


def causal_block():
    keys = lax.broadcasted_iota(jnp.int32, (ROWS, 1024), 0)
    rows = lax.broadcasted_iota(jnp.int32, (ROWS, 1024), 1)
    return keys <= jnp.bitwise_and(rows, ROWS - 1)


class Gather:
    def __init__(self, full, cut, width, ss, rs, base, dp, y, z):
        self.full, self.cut, self.width, self.ss, self.rs, self.base = full, cut, width, ss, rs, base
        self.dp, self.y, self.z = dp, y, z
        self.started = []
        self.a, self.b = pl.ds(0, cut), pl.ds(cut, width - cut)

    def copy(self, ref, k, device):
        return remote(ref, ref, self.ss.at[self.base + k], self.rs.at[self.base + k], device)

    def push(self, ref, k, device):
        copy = self.copy(ref, k, device)
        copy.start()
        self.started.append(copy)

    def seq_id(self, dy, dz):
        return {"seq": lax.rem(self.y + dy, 4) * 4 + lax.rem(self.z + dz, 4)}

    def sibling(self):
        return {"dp": 1 - self.dp}

    def region(self, phase, half, r, dp):
        y, z = lax.rem(self.y + 4 - r, 4), lax.rem(self.z + 4 - r, 4)
        if phase == 0:
            if half == 0:
                return self.full.at[dp, y, self.z, :, self.a]
            return self.full.at[dp, self.y, z, :, self.b]
        if half == 0:
            return self.full.at[dp, :, z, :, self.a]
        return self.full.at[dp, y, :, :, self.b]

    def first(self):
        for r in (1, 3, 2):
            self.push(self.region(0, 0, 0, self.dp), r - 1, self.seq_id(r, 0))
            self.push(self.region(0, 1, 0, self.dp), 3 + r - 1, self.seq_id(0, r))
        self.push(self.full.at[self.dp, self.y, self.z], 12, self.sibling())

    def take(self, phase, rounds):
        here = {"seq": self.y * 4 + self.z}
        for r in rounds:
            for half in (0, 1):
                k = 6 * phase + 3 * half + r - 1
                region = self.region(phase, half, r, self.dp)
                self.copy(region, k, here).wait_recv()
                self.push(region, (13 if phase == 0 else 19) + 3 * half + r - 1, self.sibling())

    def second(self):
        for r in (1, 3, 2):
            self.push(self.region(1, 0, 0, self.dp), 6 + r - 1, self.seq_id(0, r))
            self.push(self.region(1, 1, 0, self.dp), 9 + r - 1, self.seq_id(r, 0))

    def take_sibling(self):
        other = 1 - self.dp
        self.copy(self.full.at[other, self.y, self.z], 12, self.sibling()).wait_recv()
        for phase in (0, 1):
            for r in (1, 3, 2):
                for half in (0, 1):
                    k = (13 if phase == 0 else 19) + 3 * half + r - 1
                    self.copy(self.region(phase, half, r, other), k, self.sibling()).wait_recv()

    def finish(self):
        for copy in self.started:
            copy.wait_send()


class Scatter:
    def __init__(self, grad, landing, cut, width, halves, result, ss, rs, base, dp, y, z):
        self.grad, self.landing, self.cut, self.width, self.halves = grad, landing, cut, width, halves
        self.result, self.ss, self.rs, self.base = result, ss, rs, base
        self.dp, self.y, self.z = dp, y, z
        self.pairs, self.firsts, self.seconds = [], [], []
        self.a, self.b = pl.ds(0, cut), pl.ds(cut, width - cut)

    def copy(self, src, dst, k, device):
        made = remote(src, dst, self.ss.at[self.base + k], self.rs.at[self.base + k], device)
        made.start()
        return made

    def seq_id(self, dy, dz):
        return {"seq": lax.rem(self.y + dy, 4) * 4 + lax.rem(self.z + dz, 4)}

    def pair(self, i):
        rows = pl.ds(2 * i, 2)
        self.pairs.append(
            self.copy(
                self.grad.at[1 - self.dp, rows], self.landing.at[rows], 12 + i, {"dp": 1 - self.dp}
            )
        )

    def first(self):
        wait(self.pairs)

        def add(i, carry):
            y, z = lax.div(i, 4), lax.rem(i, 4)
            self.grad[self.dp, y, z] = (
                self.grad[self.dp, y, z].astype(f32) + self.landing[y, z].astype(f32)
            ).astype(bf16)
            return carry

        lax.fori_loop(0, 16, add, 0)
        for r in (2, 1, 3):
            y, z = lax.rem(self.y + r, 4), lax.rem(self.z + r, 4)
            self.firsts.append(
                self.copy(
                    self.grad.at[self.dp, :, z, :, self.a],
                    self.halves[0][0].at[r - 1],
                    r - 1,
                    self.seq_id(0, r),
                )
            )
            self.firsts.append(
                self.copy(
                    self.grad.at[self.dp, y, :, :, self.b],
                    self.halves[1][0].at[r - 1],
                    3 + r - 1,
                    self.seq_id(r, 0),
                )
            )

    def second(self):
        wait(self.firsts)
        for m in (0, 1):
            arrived, kept, last = self.halves[m]

            def add(i, carry):
                if m == 0:
                    mine = self.grad[self.dp, i, self.z, :, 0 : self.cut]
                else:
                    mine = self.grad[self.dp, self.y, i, :, self.cut : self.width]
                summed = mine.astype(f32)
                for r in range(3):
                    summed += arrived[r, i].astype(f32)
                kept[i] = summed.astype(bf16)
                return carry

            lax.fori_loop(0, 4, add, 0)
            for r in (2, 1, 3):
                to = lax.rem((self.y if m == 0 else self.z) + r, 4)
                target = self.seq_id(r, 0) if m == 0 else self.seq_id(0, r)
                self.seconds.append(
                    self.copy(kept.at[to], last.at[r - 1], 6 + 3 * m + r - 1, target)
                )

    def finish(self):
        wait(self.seconds)
        for m in (0, 1):
            arrived, kept, last = self.halves[m]
            summed = kept[self.y if m == 0 else self.z].astype(f32)
            for r in range(3):
                summed += last[r].astype(f32)
            if m == 0:
                self.result[:, 0 : self.cut] = summed
            else:
                self.result[:, self.cut : self.width] = summed


def block_kernel(
    x, dy, qw, kvw, ow, guw, dw, ng, hg, base_cs, block_cs,
    out, ig16, fa, ff, norm_grad, head_grad,
    wa, wf, ga, gf, ra, rf, a_in0, a_in1, f_in0, f_in1, a_k0, a_k1, f_k0, f_k1, a_l0, a_l1, f_l0, f_l1,
    h1, h1t, qkt, qpad, q_nat, kv, o16, lse, h2, hres, gains, acc, delta, dot_pad, do_nat, dq, dkv, dkv_in,
    z_, dg, du, dyt, h2t, dres16, dres, part_a, land_a, part_d, land_d, part_o, land_o, part_h, land_h,
    small, stage, small_in, turned,
    wss, wrs, gss, grs, kss, krs, bss, brs, ts, tr, mss, mrs,
):
    dp = lax.axis_index("dp")
    si = lax.axis_index("seq")
    ti = lax.axis_index("tensor")
    y, z = lax.div(si, 4), lax.rem(si, 4)
    rows = own_rows(ti)
    sibling = {"dp": 1 - dp}

    barrier = pltpu.get_barrier_semaphore()
    for r in (1, 2, 3):
        pl.semaphore_signal(
            barrier, inc=1, device_id={"tensor": lax.rem(ti + r, 4)}, device_id_type=MESH
        )
    pl.semaphore_signal(barrier, inc=1, device_id=sibling, device_id_type=MESH)

    def greet(r, carry):
        pl.semaphore_signal(
            barrier, inc=1, device_id={"seq": lax.rem(si + r, 16)}, device_id_type=MESH
        )
        return carry

    lax.fori_loop(1, 16, greet, 0)

    wa[dp, y, z, :, 0:256] = qw[...].astype(bf16)
    wa[dp, y, z, :, 256:384] = kvw[:, 0, :].astype(bf16)
    wa[dp, y, z, :, 384:512] = kvw[:, 1, :].astype(bf16)
    wa[dp, y, z, :, 512:768] = ow[...].astype(bf16)
    line = lax.broadcasted_iota(jnp.int32, (128, 32), 0)
    wa[dp, y, z, :, 768:896] = jnp.where(
        line == 0, ng[0:1], jnp.where(line == 1, ng[1:2], 0.0)
    ).T.astype(bf16)
    pl.semaphore_wait(barrier, 19)
    weights_a = Gather(wa, SPLIT_A, CA, wss, wrs, 0, dp, y, z)
    weights_f = Gather(wf, SPLIT_F, CF, wss, wrs, 25, dp, y, z)
    weights_a.first()
    wf[dp, y, z, :, 0:FFC] = guw[:, 0, :].astype(bf16)
    wf[dp, y, z, :, FFC : 2 * FFC] = guw[:, 1, :].astype(bf16)
    wf[dp, y, z, :, 2 * FFC : 3 * FFC] = dw[...].astype(bf16)
    weights_a.take(0, (1, 3, 2))
    weights_a.second()
    weights_f.first()

    x32 = x[...].astype(f32)
    h1_scale = x32 * lax.rsqrt(jnp.mean(x32 * x32, axis=-1, keepdims=True) + norm_eps)
    dyt[...] = transposed(dy[...], bf16)
    lanes = lax.broadcasted_iota(jnp.int32, (64, 128), 1)
    turn = jnp.sum(jnp.where(lanes == si, block_cs[...], 0.0), axis=1, keepdims=True)
    cos_b, sin_b = turn[0:32], turn[32:64]
    cos_t, sin_t = base_cs[0:32], base_cs[32:64]
    cosine = cos_t * cos_b - sin_t * sin_b
    sine = sin_t * cos_b + cos_t * sin_b
    square = lax.broadcasted_iota(jnp.int32, (64, 64), 0) == lax.broadcasted_iota(
        jnp.int32, (64, 64), 1
    )
    q_gain = jnp.sum(jnp.where(square, hg[0:1], 0.0), axis=1, keepdims=True)
    k_gain = jnp.sum(jnp.where(square, hg[1:2], 0.0), axis=1, keepdims=True)

    weights_a.take(1, (1, 3, 2))
    weights_a.take_sibling()

    def columns_a(lo, hi):
        return wa[:, :, :, :, lo:hi].reshape(1024, hi - lo)

    gains[...] = columns_a(768, 896).astype(f32).T[0:8]
    h1[...] = (h1_scale * gains[0:1]).astype(bf16)
    qkv = dot_nn(h1[...], columns_a(0, 512))
    qk = qkv[:, 0:384].T
    qkt[...] = qk
    rotated = []
    for h in (4, 5, 0, 1, 2, 3):
        one = qk[64 * h : 64 * h + 64]
        hat = one * lax.rsqrt(jnp.mean(one * one, axis=0, keepdims=True) + norm_eps)
        scaled = hat * (q_gain if h < 4 else k_gain)
        a, b = scaled[0:32], scaled[32:64]
        rotated += [a * cosine - b * sine, b * cosine + a * sine]
    kv[si, :, 0:128] = jnp.concatenate(rotated[0:4], axis=0).T.astype(bf16)
    kv[si, :, 128:256] = qkv[:, 384:512].astype(bf16)

    def send_kv(r):
        return remote(kv.at[si], kv.at[si], kss.at[r], krs.at[r], {"seq": si + r})

    def send_one(r, carry):
        send_kv(r).start()
        return carry

    lax.fori_loop(1, 16 - si, send_one, 0)
    qpad[...] = head_stack(jnp.concatenate(rotated[4:12], axis=0).astype(bf16))
    ones = jnp.ones((16, ROWS), bf16)
    weights_f.take(0, (1, 3, 2))

    def visit_forward(block, diagonal):
        k16 = kv[block, :, 0:128]
        p = jnp.exp2(dot_nn(k16, qpad[...]) * (SCALE * LOG2E))
        if diagonal:
            p = jnp.where(causal_block(), p, 0.0)
        p16 = p.astype(bf16)
        vt = transposed(kv[block, :, 128:256], bf16)
        for j in range(2):
            lhs = jnp.concatenate([vt[64 * j : 64 * j + 64], ones], axis=0)
            product = dot_nn(lhs, p16[:, 512 * j : 512 * j + 512])
            if diagonal:
                acc[j] = product
            else:
                acc[j] += product

    visit_forward(si, True)

    def later_forward(r, carry):
        block = si - r
        remote(kv.at[block], kv.at[block], kss.at[r], krs.at[r], {"seq": block}).wait_recv()
        visit_forward(block, False)
        return carry

    lax.fori_loop(1, si + 1, later_forward, 0)
    weights_f.second()
    pieces = []
    for j in range(2):
        total = acc[j, 64:65]
        piece = acc[j, 0:64] / total
        lse[j : j + 1] = jnp.log(total) * LOG2E
        pieces += [piece[:, 0:256], piece[:, 256:512]]
    o16[...] = jnp.concatenate(pieces, axis=0).T.astype(bf16)
    part_a[...] = dot_nt(o16[...], columns_a(512, 768)).astype(bf16)
    copies = scatter_copies(part_a, land_a, ts, tr, 0, ti)
    start(copies)
    h1t[...] = transposed(h1[...], bf16)
    q_nat[...] = transposed(qpad[...], bf16)
    wait(copies)
    mid = x[rows].astype(f32) + part_a[rows].astype(f32)
    for r in range(3):
        mid += land_a[r].astype(f32)
    hres[...] = mid
    inverse = lax.rsqrt(jnp.mean(mid * mid, axis=-1, keepdims=True) + norm_eps)
    h2[rows] = (mid * inverse * gains[1:2]).astype(bf16)
    start(gather_copies(h2, ts, tr, 3, ti))
    weights_f.take(1, (1, 3, 2))
    gather_waits(h2, ts, tr, 3, ti)
    h2t[...] = transposed(h2[...], bf16)
    weights_f.take_sibling()

    width = 384

    def columns_f(at, count):
        return wf[:, :, :, :, pl.ds(at, count)].reshape(1024, count)

    def hidden(c, carry):
        at = pl.multiple_of(c * width, 128)
        gate = dot_nn(h2[...], columns_f(at, width))
        up = dot_nn(h2[...], columns_f(at + FFC, width))
        dz = dot_nn(dy[...], columns_f(at + 2 * FFC, width))
        sigma = jax.nn.sigmoid(gate)
        silu = gate * sigma
        z_[:, pl.ds(at, width)] = (silu * up).astype(bf16)
        dg[:, pl.ds(at, width)] = (dz * up * sigma * (1.0 + gate * (1.0 - sigma))).astype(bf16)
        du[:, pl.ds(at, width)] = (dz * silu).astype(bf16)
        return carry

    lax.fori_loop(0, 3, hidden, 0)

    def rows_f(n, lo, hi):
        return wf[lax.div(n, 2), pl.ds(lax.rem(n, 2) * 2, 2), :, :, lo:hi].reshape(256, hi - lo)

    def back_d(n, carry):
        at = pl.ds(pl.multiple_of(n * 256, 256), 256)
        part_d[:, at] = (
            dot_nt(dg[...], rows_f(n, 0, FFC)) + dot_nt(du[...], rows_f(n, FFC, 2 * FFC))
        ).astype(bf16)
        return carry

    lax.fori_loop(0, 4, back_d, 0)
    copies_d = scatter_copies(part_d, land_d, ts, tr, 6, ti)
    start(copies_d)
    halves_a = ((a_in0, a_k0, a_l0), (a_in1, a_k1, a_l1))
    halves_f = ((f_in0, f_k0, f_l0), (f_in1, f_k1, f_l1))
    grads_a = Scatter(ga, ra, SPLIT_G, CG, halves_a, fa, gss, grs, 0, dp, y, z)
    grads_f = Scatter(gf, rf, SPLIT_F, CF, halves_f, ff, gss, grs, 14, dp, y, z)

    def grad_rows(owner, i):
        at = pl.ds(pl.multiple_of((2 * owner + i) * 256, 256), 256)
        for k, (left, right) in enumerate(((h2t, dg), (h2t, du), (dyt, z_))):
            value = dot_nn(left[at], right[...]).astype(bf16)
            gf[owner, 2 * i : 2 * i + 2, :, :, k * FFC : (k + 1) * FFC] = value.reshape(
                2, 4, 32, FFC
            )

    for i in range(2):
        grad_rows(1 - dp, i)
        grads_f.pair(i)
    for i in range(2):
        grad_rows(dp, i)

    def back_o(n, carry):
        at = pl.ds(pl.multiple_of(n * 256, 256), 256)
        part_o[:, at] = dot_nt(z_[...], rows_f(n, 2 * FFC, 3 * FFC)).astype(bf16)
        return carry

    lax.fori_loop(0, 4, back_o, 0)
    wait(copies_d)
    dh2 = part_d[rows].astype(f32)
    for r in range(3):
        dh2 += land_d[r].astype(f32)
    mid = hres[...]
    inverse = lax.rsqrt(jnp.mean(mid * mid, axis=-1, keepdims=True) + norm_eps)
    normed = mid * inverse
    scaled = dh2 * gains[1:2]
    inner = jnp.mean(scaled * normed, axis=-1, keepdims=True)
    grad = dy[rows].astype(f32) + inverse * (scaled - normed * inner)
    dres[...] = grad
    dres16[rows] = grad.astype(bf16)
    start(gather_copies(dres16, ts, tr, 9, ti))
    norm_two = jnp.sum(dh2 * normed, axis=0, keepdims=True)
    grads_f.first()
    copies_o = scatter_copies(part_o, land_o, ts, tr, 12, ti)
    gather_waits(dres16, ts, tr, 9, ti)
    start(copies_o)

    do_t = transposed(dot_nn(dres16[...], columns_a(512, 768)).astype(bf16), f32)
    products = do_t * transposed(o16[...], f32)
    sums = [jnp.sum(products[64 * h : 64 * h + 64], axis=0, keepdims=True) for h in range(4)]
    delta[...] = jnp.concatenate(sums, axis=1)
    dot_pad[...] = head_stack(do_t.astype(bf16))
    do_nat[...] = transposed(dot_pad[...], bf16)

    def visit_backward(block, diagonal):
        k16 = kv[block, :, 0:128]
        kt = transposed(k16, bf16)
        shift = jnp.concatenate([lse[0:1], lse[1:2]], axis=1)
        p = jnp.exp2(dot_nn(k16, qpad[...]) * (SCALE * LOG2E) - shift)
        if diagonal:
            p = jnp.where(causal_block(), p, 0.0)
        dprob = dot_nn(kv[block, :, 128:256], dot_pad[...])
        ds16 = (p * (dprob - delta[...])).astype(bf16)
        dkv[block, :, 0:128] = (dot_nn(ds16, q_nat[...]) * SCALE).astype(bf16)
        dkv[block, :, 128:256] = dot_nn(p.astype(bf16), do_nat[...]).astype(bf16)
        for j in range(2):
            product = dot_nn(kt[64 * j : 64 * j + 64], ds16[:, 512 * j : 512 * j + 512])
            if diagonal:
                dq[j] = product
            else:
                dq[j] += product

    visit_backward(si, True)

    def send_dkv(r):
        return remote(dkv.at[si - r], dkv_in.at[r], bss.at[r], brs.at[r], {"seq": si - r})

    def later_backward(r, carry):
        visit_backward(si - r, False)
        send_dkv(r).start()
        return carry

    lax.fori_loop(1, si + 1, later_backward, 0)

    wait(copies_o)
    ffn = part_o[rows].astype(f32)
    for r in range(3):
        ffn += land_o[r].astype(f32)
    out[rows] = (hres[...] + ffn).astype(bf16)
    start(gather_copies(out, ts, tr, 15, ti))
    hats, inverses = [], []
    for h in range(6):
        one = qkt[64 * h : 64 * h + 64]
        inverse = lax.rsqrt(jnp.mean(one * one, axis=0, keepdims=True) + norm_eps)
        inverses.append(inverse)
        hats.append(one * inverse)

    def head_back(gradient, h):
        a, b = gradient[0:32], gradient[32:64]
        normed = jnp.concatenate([a * cosine + b * sine, b * cosine - a * sine], axis=0)
        scaled = normed * (q_gain if h < 4 else k_gain)
        inner = jnp.mean(scaled * hats[h], axis=0, keepdims=True)
        return inverses[h] * (scaled - hats[h] * inner), normed * hats[h]

    results, q_products = [], 0.0
    for h in range(4):
        piece = dq[h // 2, :, 256 * (h % 2) : 256 * (h % 2) + 256] * SCALE
        result, product = head_back(piece, h)
        results.append(result)
        q_products = q_products + product
    grad_o = dot_nn(transposed(dres16[...], bf16), o16[...]).astype(bf16)
    ga[:, :, :, :, 512:768] = grad_o.reshape(2, 4, 4, 32, 256)

    def receive(r, total):
        remote(dkv.at[si], dkv_in.at[r], bss.at[r], brs.at[r], {"seq": si}).wait_recv()
        return total + dkv_in[r].astype(f32)

    total = lax.fori_loop(1, 16 - si, receive, dkv[si].astype(f32))
    dkt = total[:, 0:128].T
    k_products = 0.0
    for h in range(2):
        result, product = head_back(dkt[64 * h : 64 * h + 64], 4 + h)
        results.append(result)
        k_products = k_products + product
    dqk = jnp.concatenate(results, axis=0).T.astype(bf16)
    dqkv = jnp.concatenate([dqk, total[:, 128:256].astype(bf16)], axis=1)
    grad_qkv = dot_nn(h1t[...], dqkv).astype(bf16)
    ga[:, :, :, :, 0:512] = grad_qkv.reshape(2, 4, 4, 32, 512)
    for i in range(2):
        grads_a.pair(i)
    part_h[...] = dot_nt(dqkv, columns_a(0, 512)).astype(bf16)
    copies_h = scatter_copies(part_h, land_h, ts, tr, 18, ti)
    start(copies_h)
    blank = jnp.zeros((1, 960), f32)
    head_rows = [
        jnp.concatenate([jnp.sum(q_products.T, axis=0, keepdims=True), blank], axis=1),
        jnp.concatenate([jnp.sum(k_products.T, axis=0, keepdims=True), blank], axis=1),
    ]
    grads_f.second()
    grads_a.first()
    wait(copies_h)
    dh1 = part_h[rows].astype(f32)
    for r in range(3):
        dh1 += land_h[r].astype(f32)
    own_x = x[rows].astype(f32)
    inverse = lax.rsqrt(jnp.mean(own_x * own_x, axis=-1, keepdims=True) + norm_eps)
    normed = own_x * inverse
    norm_one = jnp.sum(dh1 * normed, axis=0, keepdims=True)
    small[0] = jnp.concatenate([norm_one, norm_two] + head_rows + [jnp.zeros((4, 1024), f32)], axis=0)
    small_x = [
        remote(
            small.at[0], small.at[r], mss.at[r - 1], mrs.at[r - 1], {"tensor": lax.rem(ti + r, 4)}
        )
        for r in (1, 2, 3)
    ]
    start(small_x)
    scaled = dh1 * gains[0:1]
    inner = jnp.mean(scaled * normed, axis=-1, keepdims=True)
    ig16[rows] = (dres[...] + inverse * (scaled - normed * inner)).astype(bf16)
    start(gather_copies(ig16, ts, tr, 21, ti))
    wait(small_x)
    stage[0] = small[0] + small[1] + small[2] + small[3]
    small_c = [remote(stage.at[0], small_in.at[0], mss.at[3], mrs.at[3], sibling)]
    start(small_c)
    grads_a.second()
    wait(small_c)
    stage[1] = stage[0] + small_in[0]
    small_z = [
        remote(
            stage.at[1], small_in.at[r], mss.at[3 + r], mrs.at[3 + r],
            {"seq": y * 4 + lax.rem(z + r, 4)},
        )
        for r in (1, 2, 3)
    ]
    start(small_z)
    grads_f.finish()
    wait(small_z)
    stage[2] = stage[1] + small_in[1] + small_in[2] + small_in[3]
    small_y = [
        remote(
            stage.at[2], small_in.at[3 + r], mss.at[6 + r], mrs.at[6 + r],
            {"seq": lax.rem(y + r, 4) * 4 + z},
        )
        for r in (1, 2, 3)
    ]
    start(small_y)
    grads_a.finish()
    wait(small_y)
    summed = stage[2] + small_in[4] + small_in[5] + small_in[6]
    head_grad[...] = summed[2:4, 0:64]
    turned[...] = jnp.concatenate([summed, jnp.zeros((120, 1024), f32)], axis=0).T
    mine = turned[pl.ds(pl.multiple_of((dp * 16 + si) * 32, 32), 32), :]
    norm_grad[...] = mine.T[0:2]

    def kv_done(r, carry):
        send_kv(r).wait_send()
        return carry

    lax.fori_loop(1, 16 - si, kv_done, 0)

    def dkv_done(r, carry):
        send_dkv(r).wait_send()
        return carry

    lax.fori_loop(1, si + 1, dkv_done, 0)
    weights_a.finish()
    weights_f.finish()
    gather_waits(out, ts, tr, 15, ti)
    gather_waits(ig16, ts, tr, 21, ti)


def block_step(*operands):
    def b(*shape):
        return pltpu.VMEM(shape, bf16)

    def f(*shape):
        return pltpu.VMEM(shape, f32)

    def s(count):
        return pltpu.SemaphoreType.DMA((count,))

    rest_a, rest_f = CG - SPLIT_G, CF - SPLIT_F
    return pl.pallas_call(
        block_kernel,
        out_shape=(
            jax.ShapeDtypeStruct((256, 1024), bf16),
            jax.ShapeDtypeStruct((256, 1024), bf16),
            jax.ShapeDtypeStruct((32, CG), f32),
            jax.ShapeDtypeStruct((32, CF), f32),
            jax.ShapeDtypeStruct((2, 32), f32),
            jax.ShapeDtypeStruct((2, 64), f32),
        ),
        in_specs=[VMEM] * len(operands),
        out_specs=(VMEM,) * 6,
        scratch_shapes=[
            b(2, 4, 4, 32, CA), b(2, 4, 4, 32, CF), b(2, 4, 4, 32, CG), b(2, 4, 4, 32, CF),
            b(4, 4, 32, CG), b(4, 4, 32, CF),
            b(3, 4, 32, SPLIT_G), b(3, 4, 32, rest_a), b(3, 4, 32, SPLIT_F), b(3, 4, 32, rest_f),
            b(4, 32, SPLIT_G), b(4, 32, rest_a), b(4, 32, SPLIT_F), b(4, 32, rest_f),
            b(3, 32, SPLIT_G), b(3, 32, rest_a), b(3, 32, SPLIT_F), b(3, 32, rest_f),
            b(256, 1024), b(1024, 256), f(384, 256), b(128, 1024), b(1024, 128), b(16, 256, 256),
            b(256, 256), f(2, 512), b(256, 1024), f(64, 1024), f(8, 1024), f(2, 80, 512), f(1, 1024),
            b(128, 1024), b(1024, 128), f(2, 64, 512), b(16, 256, 256), b(16, 256, 256),
            b(256, FFC), b(256, FFC), b(256, FFC), b(1024, 256), b(1024, 256), b(256, 1024), f(64, 1024),
            b(256, 1024), b(3, 64, 1024), b(256, 1024), b(3, 64, 1024),
            b(256, 1024), b(3, 64, 1024), b(256, 1024), b(3, 64, 1024),
            f(4, 8, 1024), f(3, 8, 1024), f(7, 8, 1024), f(1024, 128),
            s(50), s(50), s(28), s(28), s(16), s(16), s(16), s(16), s(24), s(24), s(10), s(10),
        ],
        compiler_params=params(1, 62),
        name="block_step",
    )(*operands)


def adamw(weight, momentum, variance, gradient, decay):
    first = beta_one * momentum + (1.0 - beta_one) * gradient
    second = beta_two * variance + (1.0 - beta_two) * gradient * gradient
    first_fixed = first / (1.0 - beta_one**adam_count)
    second_fixed = second / (1.0 - beta_two**adam_count)
    direction = first_fixed / (jnp.sqrt(second_fixed) + adam_eps) + decay * weight
    return (direction, first, second)


def adam_kernel(*refs):
    fa, ff, norm_grad, head_grad = refs[0:4]
    weights, momenta, variances = refs[4:11], refs[11:18], refs[18:25]
    grads, directions, firsts, seconds = refs[25:32], refs[32:39], refs[39:46], refs[46:53]
    grads[0][...] = fa[:, 0:256]
    grads[1][:, 0, :] = fa[:, 256:384]
    grads[1][:, 1, :] = fa[:, 384:512]
    grads[2][...] = fa[:, 512:768]
    grads[3][:, 0, :] = ff[:, 0:FFC]
    grads[3][:, 1, :] = ff[:, FFC : 2 * FFC]
    grads[4][...] = ff[:, 2 * FFC : 3 * FFC]
    grads[5][...] = norm_grad[...]
    grads[6][...] = head_grad[...]
    for n in range(7):
        direction, first, second = adamw(
            weights[n][...],
            momenta[n][...],
            variances[n][...],
            grads[n][...],
            decay_rate if n < 5 else 0.0,
        )
        directions[n][...] = direction
        firsts[n][...] = first
        seconds[n][...] = second


def adam_step(found, weights, momenta, variances):
    shapes = tuple(jax.ShapeDtypeStruct(w.shape, f32) for w in weights)
    return pl.pallas_call(
        adam_kernel,
        out_shape=shapes * 4,
        in_specs=[VMEM] * 25,
        out_specs=(VMEM,) * 28,
        compiler_params=pltpu.CompilerParams(vmem_limit_bytes=40 * 1024 * 1024),
        name="adam_step",
    )(*found, *weights, *momenta, *variances)


def rope_constants():
    frequency = rope_base ** (-(np.arange(HD // 2, dtype=np.float64) * 2.0) / HD)
    base = frequency[:, None] * np.arange(ROWS)[None, :]
    block = frequency[:, None] * (ROWS * np.arange(128) * (np.arange(128) < 16))[None, :]
    return tuple(
        np.concatenate([np.cos(a), np.sin(a)], axis=0).astype(np.float32) for a in (base, block)
    )


def body(
    block_input,
    upstream_grad,
    query_weight,
    key_value_weight,
    output_weight,
    gateup_weight,
    down_weight,
    norm_gains,
    head_norm_gains,
    query_momentum,
    query_variance,
    key_value_momentum,
    key_value_variance,
    output_momentum,
    output_variance,
    gateup_momentum,
    gateup_variance,
    down_momentum,
    down_variance,
    norm_momentum,
    norm_variance,
    head_momentum,
    head_variance,
):
    base_cs, block_cs = rope_constants()
    weights = (
        query_weight, key_value_weight, output_weight, gateup_weight, down_weight, norm_gains.T,
        head_norm_gains,
    )
    momenta = (
        query_momentum, key_value_momentum, output_momentum, gateup_momentum, down_momentum,
        norm_momentum.T, head_momentum,
    )
    variances = (
        query_variance, key_value_variance, output_variance, gateup_variance, down_variance,
        norm_variance.T, head_variance,
    )
    out, ig16, *found = block_step(
        block_input[0], upstream_grad[0], *weights, jnp.asarray(base_cs), jnp.asarray(block_cs)
    )
    results = adam_step(found, weights, momenta, variances)
    grads, directions, firsts, seconds = (
        [v.T if n == 5 else v for n, v in enumerate(results[7 * i : 7 * i + 7])] for i in range(4)
    )
    moments = [v for pair in zip(firsts, seconds) for v in pair]
    return (out[None], ig16.astype(f32)[None], *grads, *directions, *moments)


def solution(mesh):
    in_specs = (
        P("dp", "seq", None),
        P("dp", "seq", None),
        P(("dp", "seq"), "tensor"),
        P(("dp", "seq"), None, "tensor"),
        P(("dp", "seq"), "tensor"),
        P(("dp", "seq"), None, "tensor"),
        P(("dp", "seq"), "tensor"),
        P(("dp", "seq"), None),
        P(),
        P(("dp", "seq"), "tensor"),
        P(("dp", "seq"), "tensor"),
        P(("dp", "seq"), None, "tensor"),
        P(("dp", "seq"), None, "tensor"),
        P(("dp", "seq"), "tensor"),
        P(("dp", "seq"), "tensor"),
        P(("dp", "seq"), None, "tensor"),
        P(("dp", "seq"), None, "tensor"),
        P(("dp", "seq"), "tensor"),
        P(("dp", "seq"), "tensor"),
        P(("dp", "seq"), None),
        P(("dp", "seq"), None),
        P(),
        P(),
    )
    out_specs = (
        P("dp", "seq", None),
        P("dp", "seq", None),
        P(("dp", "seq"), "tensor"),
        P(("dp", "seq"), None, "tensor"),
        P(("dp", "seq"), "tensor"),
        P(("dp", "seq"), None, "tensor"),
        P(("dp", "seq"), "tensor"),
        P(("dp", "seq"), None),
        P(),
        P(("dp", "seq"), "tensor"),
        P(("dp", "seq"), None, "tensor"),
        P(("dp", "seq"), "tensor"),
        P(("dp", "seq"), None, "tensor"),
        P(("dp", "seq"), "tensor"),
        P(("dp", "seq"), None),
        P(),
        P(("dp", "seq"), "tensor"),
        P(("dp", "seq"), "tensor"),
        P(("dp", "seq"), None, "tensor"),
        P(("dp", "seq"), None, "tensor"),
        P(("dp", "seq"), "tensor"),
        P(("dp", "seq"), "tensor"),
        P(("dp", "seq"), None, "tensor"),
        P(("dp", "seq"), None, "tensor"),
        P(("dp", "seq"), "tensor"),
        P(("dp", "seq"), "tensor"),
        P(("dp", "seq"), None),
        P(("dp", "seq"), None),
        P(),
        P(),
    )
    return jax.shard_map(body, mesh=mesh, in_specs=in_specs, out_specs=out_specs, check_vma=False)
```
